32 devices in a mesh: dp: 8 (over y, x, core), tensor: 4 (over z).
Axes of the slice: x: 2, y: 2, z: 4, core: 2. Of those that a mesh axis runs over, the one named last changes fastest.
Arguments:
- tokens: bfloat16 [30720, 512], P(('dp', 'tensor')), may hold values from -6 to 6
- cotangent: bfloat16 [30720, 512], P(('dp', 'tensor')), may hold values from -6 to 6
- lengths: int32 [32], P('dp'), may hold values from 96 to 720, as said below
- neighbours: int32 [30720, 8], P('dp'), may hold values from -1 to 3779, as said below
- ln1_gain: float32 [512], replicated, may hold values from 0.5 to 1.5
- ln1_shift: float32 [512], replicated, may hold values from -1.75 to 1.75
- w_qkv: bfloat16 [3, 512, 512], P(None, None, 'tensor'), may hold values from -0.25 to 0.25
- w_out: bfloat16 [512, 512], P('tensor'), may hold values from -0.5 to 0.5
- b_out: float32 [512], replicated, may hold values from -1.75 to 1.75
- ln2_gain: float32 [512], replicated, may hold values from 0.5 to 1.5
- ln2_shift: float32 [512], replicated, may hold values from -1.75 to 1.75
- w_up: bfloat16 [512, 2048], P(None, 'tensor'), may hold values from -0.25 to 0.25
- b_up: bfloat16 [2048], P('tensor'), may hold values from -3 to 3
- w_down: bfloat16 [2048, 512], P('tensor'), may hold values from -0.1875 to 0.1875
- b_down: float32 [512], replicated, may hold values from -1.75 to 1.75
Outputs:
- output: bfloat16 [30720, 512], P(('dp', 'tensor'))
- grad_tokens: float32 [30720, 512], P(('dp', 'tensor'))
- grad_ln1_gain: float32 [512], replicated
- grad_ln1_shift: float32 [512], replicated
- grad_w_qkv: float32 [3, 512, 512], P(None, None, 'tensor')
- grad_w_out: float32 [512, 512], P('tensor')
- grad_b_out: float32 [512], replicated
- grad_ln2_gain: float32 [512], replicated
- grad_ln2_shift: float32 [512], replicated
- grad_w_up: float32 [512, 2048], P(None, 'tensor')
- grad_b_up: float32 [2048], P('tensor')
- grad_w_down: float32 [2048, 512], P('tensor')
- grad_b_down: float32 [512], replicated
The draws below stay inside these ranges and needn't reach their ends.
Inputs may be any that keep to these rules, and one draw needn't show every extreme that they name: `lengths`: lengths are multiples of 16; among the 4 windows of each index of dp one has exactly 720 steps. `neighbours`: within a group of 3840 rows window w (of that group) step p sits at level 0 in row w * 720 + p, its level 1 node p at row 2880 + w * 180 + p and its level 2 node p at row 3600 + w * 45 + p. A live node lists, as row numbers within the group: itself, the node before and after it on its level within its window, its parent (p / 4 one level up) and its four children (4 * p to 4 * p + 3 one level down), -1 where none exists; nodes past a window's length at their level and the remaining rows list -1 only.
All inputs are finite; a program needn't handle non-finite values.
Results may differ from the reference program's by a relative error of at most 0.014.
Values may be sent and summed in bfloat16 or wider, within the bound.
No kernel may reach another device: no remote copies, remote signals or barrier semaphores. Data moves between devices by JAX's collectives and lax.ppermute only.
A program may use at most 128 MiB of HBM per device.

```python
import math
import jax
import jax.numpy as jnp
from jax import lax

D = 512
H = 8
DH = 64
FF = 2048
MAXLEN = 720
LEN_LO = 96
WIN_GRP = 4
NODES_GRP = 3840
NODES = 30720
WINDOWS = 32


def pyramid_lengths(key):
    group_count = WINDOWS // WIN_GRP
    lengths_key = jax.random.fold_in(key, 11)
    longest_key = jax.random.fold_in(key, 12)
    drawn = jax.random.randint(lengths_key, (group_count, WIN_GRP), LEN_LO // 16, MAXLEN // 16 + 1) * 16
    longest = jax.random.randint(longest_key, (group_count, 1), 0, WIN_GRP)
    slot_ids = jnp.arange(WIN_GRP, dtype=jnp.int32)[None, :]
    return jnp.where(slot_ids == longest, MAXLEN, drawn).astype(jnp.int32)


def pyramid_links(group_lengths):
    row_ids = jnp.arange(NODES_GRP, dtype=jnp.int32)
    first_end = WIN_GRP * MAXLEN
    second_end = first_end + first_end // 4
    third_end = second_end + first_end // 16
    level_id = (row_ids >= first_end).astype(jnp.int32) + (row_ids >= second_end).astype(jnp.int32) + (row_ids >= third_end).astype(jnp.int32)
    start_row = jnp.where(level_id == 0, 0, jnp.where(level_id == 1, first_end, second_end)).astype(jnp.int32)
    factor = jnp.where(level_id == 0, 1, jnp.where(level_id == 1, 4, 16)).astype(jnp.int32)
    offset = row_ids - start_row
    slot_size = MAXLEN // factor
    window = offset // slot_size
    position = offset % slot_size
    onehot = window[:, None] == jnp.arange(WIN_GRP, dtype=jnp.int32)[None, :]
    length = jnp.sum(jnp.where(onehot, group_lengths[None, :], 0), axis=1).astype(jnp.int32)
    limit = length // factor
    live = (level_id < 3) & (position < limit)
    left_row = jnp.where(position >= 1, row_ids - 1, -1)
    right_row = jnp.where(position + 1 < limit, row_ids + 1, -1)
    parent_row = jnp.where(level_id == 0, first_end + window * (MAXLEN // 4) + position // 4, jnp.where(level_id == 1, second_end + window * (MAXLEN // 16) + position // 4, -1))
    child_base = jnp.where(level_id == 1, window * MAXLEN + 4 * position, first_end + window * (MAXLEN // 4) + 4 * position)
    children = [jnp.where(level_id >= 1, child_base + child, -1) for child in range(4)]
    table = jnp.stack([row_ids, left_row, right_row, parent_row] + children, axis=1)
    return jnp.where(live[:, None], table, -1).astype(jnp.int32)


def draw_lengths(key, part):
    return pyramid_lengths(key).reshape(WINDOWS)


def draw_neighbours(key, part):
    tables = jax.vmap(pyramid_links)(pyramid_lengths(key))
    return tables.reshape(WINDOWS // WIN_GRP * NODES_GRP, 8)


def steps_of(rng, extent, cuts, smallest, high):
    gain, own = 1.0, jax.random.fold_in(rng, 6)
    for axis_at, shards_of in cuts:
        heights = jnp.exp(jax.random.uniform(jax.random.fold_in(own, axis_at), (shards_of,), jnp.float32, smallest / len(cuts), high / len(cuts)))
        gain = gain * jnp.repeat(heights, extent[axis_at] // shards_of).reshape([-1 if axis == axis_at else 1 for axis in range(len(extent))])
    return gain


def normal_values(rng, extent, deviation, most, shards=(), kind=jnp.bfloat16):
    values = jax.random.normal(rng, extent, jnp.float32) * deviation
    if len(shards) > 0:
        values = steps_of(rng, extent, shards, -0.22, 0.18) * values
    return jnp.clip(values, min=-most, max=most).astype(kind)


def setup_inputs(seed: int = 0) -> dict:
    key_of = jax.random.split(jax.random.key(seed), 16)
    return {
        "tokens": normal_values(key_of[0], (NODES, D), 1.0, 6.0, ((0, 32),)),
        "cotangent": normal_values(key_of[1], (NODES, D), 1.0, 6.0, ((0, 32),)),
        "lengths": draw_lengths(jax.random.fold_in(key_of[15], 71), 0),
        "neighbours": draw_neighbours(jax.random.fold_in(key_of[15], 71), 0),
        "ln1_gain": jnp.clip(1.0 + 0.1 * jax.random.normal(key_of[4], (D,), jnp.float32), 0.5, 1.5),
        "ln1_shift": normal_values(key_of[5], (D,), 0.3, 1.75, (), jnp.float32),
        "w_qkv": normal_values(key_of[6], (3, D, D), D ** -0.5, 0.25, ((2, 4),)),
        "w_out": normal_values(key_of[7], (D, D), (D // 4) ** -0.5, 0.5, ((0, 4),)),
        "b_out": normal_values(key_of[8], (D,), 0.3, 1.75, (), jnp.float32),
        "ln2_gain": jnp.clip(1.0 + 0.1 * jax.random.normal(key_of[9], (D,), jnp.float32), 0.5, 1.5),
        "ln2_shift": normal_values(key_of[10], (D,), 0.3, 1.75, (), jnp.float32),
        "w_up": normal_values(key_of[11], (D, FF), D ** -0.5, 0.25, ((1, 4),)),
        "b_up": normal_values(key_of[12], (FF,), 0.5, 3.0, ((0, 4),)),
        "w_down": normal_values(key_of[13], (FF, D), (FF // 2) ** -0.5, 0.1875, ((0, 4),)),
        "b_down": normal_values(key_of[14], (D,), 0.3, 1.75, (), jnp.float32),
    }


@jax.custom_vjp
def low(v):
    return lax.optimization_barrier(v.astype(jnp.bfloat16)).astype(jnp.float32)

@jax.custom_vjp
def low_back(v):
    return v

def low_keep(v):
    return (low(v), None)

def low_pass(kept, grad):
    return (grad,)

def back_keep(v):
    return (v, None)

def back_low(kept, grad):
    return (low(grad),)
low.defvjp(low_keep, low_pass)
low_back.defvjp(back_keep, back_low)

def matmul_f32(left, right):
    return jnp.dot(left, right, precision=lax.Precision.HIGHEST, preferred_element_type=jnp.float32)

def normalize(values, gain_vec, shift_vec):
    center = values - lax.optimization_barrier(jnp.mean(values, axis=-1, keepdims=True))
    spread = lax.optimization_barrier(jnp.mean(center * center, axis=-1, keepdims=True))
    return center * lax.rsqrt(spread + 1e-05) * gain_vec + shift_vec

def node_valid(group_lengths):
    row_ids = jnp.arange(NODES_GRP, dtype=jnp.int32)
    first_end = WIN_GRP * MAXLEN
    second_end = first_end + first_end // 4
    third_end = second_end + first_end // 16
    level_id = (row_ids >= first_end).astype(jnp.int32) + (row_ids >= second_end).astype(jnp.int32) + (row_ids >= third_end).astype(jnp.int32)
    start_row = jnp.where(level_id == 0, 0, jnp.where(level_id == 1, first_end, second_end)).astype(jnp.int32)
    factor = jnp.where(level_id == 0, 1, jnp.where(level_id == 1, 4, 16)).astype(jnp.int32)
    offset = row_ids - start_row
    slot_size = MAXLEN // factor
    window = offset // slot_size
    position = offset % slot_size
    onehot = window[:, None] == jnp.arange(WIN_GRP, dtype=jnp.int32)[None, :]
    length = lax.optimization_barrier(jnp.sum(jnp.where(onehot, group_lengths[None, :], 0), axis=1)).astype(jnp.int32)
    return ((level_id < 3) & (position < length // factor)).astype(jnp.float32)

def attend(queries, keys, values, links, live_rows):
    row_count = queries.shape[0]
    link_count = links.shape[1]
    present = links >= 0
    safe_index = jnp.maximum(links, 0).astype(jnp.int32)
    query_heads = queries.reshape(row_count, H, DH)
    key_rows = keys[safe_index].reshape(row_count, link_count, H, DH)
    value_rows = values[safe_index].reshape(row_count, link_count, H, DH)
    raw = jnp.einsum('rhe,rjhe->rjh', query_heads, key_rows, precision=lax.Precision.HIGHEST) * (1.0 / math.sqrt(DH))
    scores = low_back(raw)
    present_three = present[:, :, None]
    highest = lax.optimization_barrier(jnp.max(jnp.where(present_three, scores, -1000000000.0), axis=1, keepdims=True))
    anyone = jnp.any(present, axis=1)[:, None, None]
    highest = jnp.where(anyone, highest, 0.0)
    weights = jnp.where(present_three, jnp.exp(scores - highest), 0.0)
    denominator = lax.optimization_barrier(jnp.sum(weights, axis=1, keepdims=True)) + jnp.where(anyone, 0.0, 1.0)
    probability = low(weights / denominator)
    context = jnp.einsum('rjh,rjhe->rhe', probability, value_rows, precision=lax.Precision.HIGHEST)
    return context.reshape(row_count, H * DH) * live_rows[:, None]

def pyramid_layer(inputs_f32, weights_all, links, live_rows):
    ln1_gain, ln1_shift, w_qkv, w_out, b_out, ln2_gain, ln2_shift, w_up, b_up, w_down, b_down = weights_all
    normed_one = low(normalize(inputs_f32, ln1_gain, ln1_shift))
    packed = jnp.einsum('rd,ide->ire', normed_one, w_qkv, precision=lax.Precision.HIGHEST)
    packed = low(low_back(packed))
    context = attend(packed[0], packed[1], packed[2], links, live_rows)
    context = low(low_back(context))
    middle = inputs_f32 + low_back(matmul_f32(context, w_out) + b_out)
    normed_two = low(normalize(middle, ln2_gain, ln2_shift))
    up_pre = low_back(matmul_f32(normed_two, w_up) + b_up)
    activated = low(jax.nn.gelu(up_pre, approximate=True))
    return middle + low_back(matmul_f32(activated, w_down) + b_down)

def reference(tokens, cotangent, lengths, neighbours, ln1_gain, ln1_shift, w_qkv, w_out, b_out, ln2_gain, ln2_shift, w_up, b_up, w_down, b_down):
    params = tuple((weight_in.astype(jnp.float32) for weight_in in (ln1_gain, ln1_shift, w_qkv, w_out, b_out, ln2_gain, ln2_shift, w_up, b_up, w_down, b_down)))
    groups = tokens.shape[0] // NODES_GRP
    scanned = (tokens.reshape(groups, NODES_GRP, D), cotangent.reshape(groups, NODES_GRP, D), neighbours.reshape(groups, NODES_GRP, neighbours.shape[1]), lengths.reshape(groups, WIN_GRP))

    def visit(totals, group_item):
        block_in, block_grad, block_links, block_lengths = group_item
        live_rows = node_valid(block_lengths)

        def forward(inputs_f32, *weights_all):
            return pyramid_layer(inputs_f32, weights_all, block_links, live_rows)
        layer_out, pullback = jax.vjp(forward, block_in.astype(jnp.float32), *params)
        grads = pullback(block_grad.astype(jnp.float32))
        totals = tuple((running + grad_part for running, grad_part in zip(totals, grads[1:])))
        return (totals, (layer_out.astype(jnp.bfloat16), grads[0]))
    zero_grads = tuple((jnp.zeros(weight_in.shape, jnp.float32) for weight_in in params))
    totals, (outputs, grad_in) = lax.scan(visit, zero_grads, scanned)
    return (outputs.reshape(-1, D), grad_in.reshape(-1, D), totals[0], totals[1], totals[2], totals[3], totals[4], totals[5], totals[6], totals[7], totals[8], totals[9], totals[10])
```

```python
import math

import jax
import jax.numpy as jnp
import numpy as np
from jax import lax
from jax.experimental import pallas as pl
from jax.experimental.pallas import tpu as pltpu
from jax.sharding import PartitionSpec as P

D = 512
DH = 64
MAXLEN = 720
NODES_GRP = 3840
SHARD = NODES_GRP // 4
F32 = jnp.float32
BF16 = jnp.bfloat16

BLK = 48
QUAD = 4 * BLK
L1_ROW = 4 * QUAD
L2_ROW = L1_ROW + QUAD
USED = L2_ROW + BLK
ROWS = 1024
EXT_C = (0, 240, 432, 672)
EXT_LEFT = (624, 0, 240, 432)
EXT_RIGHT = (240, 432, 672, 48)
EXT_L1 = 912
EXT_L2 = 1200
EXT = 1296
VMEM_BYTES = 60 * 1024 * 1024
SEND_LO = SHARD - MAXLEN
LOW_HEAD = (0, 176, 352)
LOW_TAIL = (720, 752, 800)


def slot_rows():
    spare = [BLK * block + step for block in range(21) for step in range(45, 48)]
    level0 = [QUAD * (p % 4) + BLK * (p // 4 % 4) + p // 16 for p in range(720)]
    level1 = [L1_ROW + BLK * (p % 4) + p // 4 for p in range(180)]
    level2 = [L2_ROW + p for p in range(45)]
    return level0, level1, level2, spare


def gather_table():
    level0, level1, level2, spare = slot_rows()
    table = np.full((4, ROWS, 1), -1, np.int32)
    for t in range(4):
        for p in range(720):
            at = 720 - 240 * t + p
            table[t, level0[p], 0] = SHARD + at if at < 720 else at - 720
        for p in range(180):
            table[t, level1[p], 0] = 540 + p if t == 3 else SHARD + 720 + 180 * t - LOW_HEAD[t] + p
        for p in range(45):
            table[t, level2[p], 0] = 855 + p if t == 3 else SHARD + 720 + 192 + 720 + 45 * t - LOW_TAIL[t] + p
        if t == 3:
            for p in range(60):
                table[t, spare[p], 0] = 900 + p
    return table


def spread_table():
    level0, level1, level2, spare = slot_rows()
    table = np.full((4, SHARD, 1), -1, np.int32)
    for t in range(3):
        for i in range(SHARD):
            at = 240 * t + i
            table[t, i, 0] = level0[at] if at < 720 else ROWS + level0[at - 720]
    for i in range(SHARD):
        if i < 720:
            w, row = i // 180, level1[i % 180]
        elif i < 900:
            w, row = (i - 720) // 45, level2[(i - 720) % 45]
        else:
            w, row = 3, spare[i - 900]
        table[3, i, 0] = row if w == 3 else ROWS + 240 * w + row - L1_ROW
    return table


def dot_nn(a, b):
    return jnp.dot(a, b, preferred_element_type=F32)


def dot_nt(a, b):
    return lax.dot_general(a, b, (((1,), (1,)), ((), ())), preferred_element_type=F32)


def dot_tn(a, b):
    return lax.dot_general(a, b, (((0,), (0,)), ((), ())), preferred_element_type=F32)


def one_hot(source, base, count):
    return (source - base == lax.broadcasted_iota(jnp.int32, (source.shape[0], count), 1)).astype(BF16)


def gathered_rows(source, own, recv, low):
    total = dot_nn(one_hot(source, 0, SHARD), own)
    total = total + dot_nn(one_hot(source, SHARD, 720), recv)
    return total + dot_nn(one_hot(source, SHARD + 720, 256), low)


def moments(values):
    center = values - jnp.mean(values, axis=-1, keepdims=True)
    spread = jnp.mean(center * center, axis=-1, keepdims=True)
    rstd = lax.rsqrt(spread + 1e-05)
    return center * rstd, rstd


def head_sum_matrix():
    row = lax.broadcasted_iota(jnp.int32, (8 * D, 128), 0)
    col = lax.broadcasted_iota(jnp.int32, (8 * D, 128), 1)
    return (row // DH == col % 64).astype(BF16)


def head_spread_matrix():
    row = lax.broadcasted_iota(jnp.int32, (128, 8 * D), 0)
    col = lax.broadcasted_iota(jnp.int32, (128, 8 * D), 1)
    return (row == col // DH).astype(BF16)


def slot_max(values):
    for step in (8, 16, 32):
        values = jnp.maximum(values, pltpu.roll(values, step, 1))
    return values


def slot_sum(values):
    for step in (8, 16, 32):
        values = values + pltpu.roll(values, step, 1)
    return values


def shift_down(block):
    row = lax.broadcasted_iota(jnp.int32, block.shape, 0)
    return jnp.where(row == 0, 0.0, pltpu.roll(block, 1, 0))


def shift_up(block):
    row = lax.broadcasted_iota(jnp.int32, block.shape, 0)
    return jnp.where(row == BLK - 1, 0.0, pltpu.roll(block, BLK - 1, 0))


def extend(ext, rows):
    kind = ext.dtype
    for c in range(4):
        ext[EXT_C[c] : EXT_C[c] + QUAD, :] = rows(QUAD * c, QUAD).astype(kind)
    ext[EXT_L1 : EXT_L1 + QUAD, :] = rows(L1_ROW, QUAD).astype(kind)
    last = rows(L2_ROW, BLK)
    ext[EXT_L2 : EXT_L2 + BLK, :] = last.astype(kind)
    ext[192:240, :] = shift_up(rows(0, BLK)).astype(kind)
    ext[624:672, :] = shift_down(rows(3 * QUAD + 144, BLK)).astype(kind)
    ext[864:912, :] = shift_down(rows(L1_ROW + 144, BLK)).astype(kind)
    ext[1104:1152, :] = shift_up(rows(L1_ROW, BLK)).astype(kind)
    ext[1152:1200, :] = shift_down(last).astype(kind)
    ext[1248:1296, :] = shift_up(last).astype(kind)


def present(count, level, child, live_steps):
    row = lax.broadcasted_iota(jnp.int32, (count, 128), 0)
    slot = lax.broadcasted_iota(jnp.int32, (count, 128), 1) % 64 // 8
    step = row
    for start in (BLK, 2 * BLK, 3 * BLK):
        if start < count:
            step = jnp.where(row >= start, row - start, step)
    here = step < live_steps
    if level == 0:
        here = here & (slot < 4)
    if level == 2:
        here = here & (slot != 3)
    if level > 0 or child == 0:
        here = here & ((slot != 1) | (row > 0))
    if level > 0 or child == 3:
        here = here & ((slot != 2) | (row < count - BLK) | (step + 1 < live_steps))
    return here


def groups(ext):
    def quad(at):
        return lambda: ext[at : at + QUAD, :]

    def block(at):
        return lambda: ext[at : at + BLK, :]

    def tiled(at):
        return lambda: jnp.concatenate([ext[at : at + BLK, :]] * 4, axis=0)

    out = []
    for c in range(4):
        out.append((QUAD * c, QUAD, 0, c, [quad(EXT_C[c]), quad(EXT_LEFT[c]), quad(EXT_RIGHT[c]), quad(EXT_L1)]))
    out.append(
        (L1_ROW, QUAD, 1, 0, [quad(EXT_L1), quad(864), quad(960), tiled(EXT_L2)] + [quad(EXT_C[c]) for c in range(4)])
    )
    children = [block(EXT_L1 + BLK * d) for d in range(4)]
    out.append((L2_ROW, BLK, 2, 0, [block(EXT_L2), block(1152), block(1248), None] + children))
    return out


def attention_forward(
    scal, source, own, recv, low0, low1, low2, gain, shift, b_out, w_qkv, w_out, *rest
):
    pieces = rest[:8]
    x_out, n_out, qkv_out, prob_out, ctx_out, mid_out, w_full = rest[8:15]
    kx, vx, heads_in, heads_out = rest[15:]
    me, live_steps = scal[0], scal[1]
    for i in range(3):
        w_full[i, :, 0:128] = w_qkv[i]
    w_full[3, 0:128, :] = w_out[...]
    for e in range(8):
        piece = me ^ e
        at = pl.multiple_of(piece * 64, 64)
        for s in range(1, 4):
            for i in range(3):
                w_full[i, pl.ds(at, 64), 128 * s : 128 * s + 128] = pieces[e][s - 1, i]
            top = pl.multiple_of(128 * s + 64 * (piece % 2), 64)
            side = pl.multiple_of(128 * (piece // 2), 128)
            w_full[3, pl.ds(top, 64), pl.ds(side, 128)] = pieces[e][s - 1, 3]
    heads_in[...] = head_sum_matrix()
    heads_out[...] = head_spread_matrix()
    low = low0[...] + low1[...] + low2[...]
    for start in range(0, ROWS, 256):
        run = slice(start, start + 256)
        rows = gathered_rows(source[run, :], own[...], recv[...], low)
        x_out[run, :] = rows.astype(BF16)
        normed = (moments(rows)[0] * gain[...] + shift[...]).astype(BF16)
        n_out[run, :] = normed
        for i in range(3):
            qkv_out[i, run, :] = dot_nn(normed, w_full[i]).astype(BF16)
    extend(kx, lambda at, count: qkv_out[1, at : at + count, :].astype(F32))
    extend(vx, lambda at, count: qkv_out[2, at : at + count, :].astype(F32))
    ctx_out[USED:ROWS, :] = jnp.zeros((ROWS - USED, D), BF16)
    prob_out[USED:ROWS, :] = jnp.zeros((ROWS - USED, 128), F32)
    for (first, count, level, child, keys), (_, _, _, _, values) in zip(groups(kx), groups(vx)):
        query = qkv_out[0, first : first + count, :].astype(F32) * (1.0 / math.sqrt(DH))
        slots = [s for s in range(len(keys)) if keys[s] is not None]
        score = jnp.zeros((count, 128), F32)
        for s in slots:
            score = score + dot_nn((query * keys[s]()).astype(BF16), heads_in[D * s : D * s + D, :])
        here = present(count, level, child, live_steps)
        score = jnp.where(here, score, -1000000000.0)
        weight = jnp.where(here, jnp.exp(score - slot_max(score)), 0.0)
        prob = weight / jnp.maximum(slot_sum(weight), 1.0)
        prob_out[first : first + count, :] = prob
        prob_low = prob.astype(BF16)
        context = jnp.zeros((count, D), F32)
        for s in slots:
            context = context + dot_nn(prob_low, heads_out[:, D * s : D * s + D]) * values[s]()
        ctx_out[first : first + count, :] = context.astype(BF16)
    for start in range(0, ROWS, 256):
        run = slice(start, start + 256)
        mid_out[run, :] = x_out[run, :].astype(F32) + dot_nn(ctx_out[run, :], w_full[3]) + b_out[...]


def feed_forward(
    scal, source, own, recv, low0, low1, low2, mid, gain, shift, b_down, w_up, b_up, w_down, *rest
):
    pieces = rest[:8]
    y_quad, y_low, keep, send, gmid, small, small_up = rest[8:15]
    up_w, down_w, bias, normed, grad, act_s, gup_s, total, gnorm, tmp = rest[15:]
    me = scal[0]
    up_w[0] = w_up[...]
    down_w[0] = w_down[...]
    bias[0:1, :] = b_up[...].astype(F32)
    for e in range(8):
        at = pl.multiple_of((me ^ e) * 64, 64)
        for s in range(1, 4):
            up_w[s, pl.ds(at, 64), :] = pieces[e][s - 1, 0:64, :]
            down_w[s, pl.ds(at, 64), :] = pieces[e][s - 1, 64:128, :]
    for s in range(1, 4):
        bias[s : s + 1, :] = pieces[0][s - 1, 128:129, :].astype(F32)
    low = low0[...] + low1[...] + low2[...]
    for start in range(0, ROWS, 256):
        run = slice(start, start + 256)
        normed[run, :] = (moments(mid[run, :])[0] * gain[...] + shift[...]).astype(BF16)
        grad[run, :] = gathered_rows(source[run, :], own[...], recv[...], low).astype(BF16)
    total[...] = jnp.zeros_like(total)
    gnorm[...] = jnp.zeros_like(gnorm)

    def hidden(s, carry):
        up_here, down_here = up_w[s], down_w[s]
        grad_bias = jnp.zeros((1, D), F32)
        for start in range(0, ROWS, 256):
            run = slice(start, start + 256)
            pre = dot_nn(normed[run, :], up_here) + bias[pl.ds(s, 1), :]
            square = pre * pre
            root = math.sqrt(2.0 / math.pi)
            bent = jnp.tanh(pre * (root + (root * 0.044715) * square))
            half = 0.5 * pre
            act = (half + half * bent).astype(BF16)
            slope = (0.5 + 0.5 * bent) + half * (1.0 - bent * bent) * (root + (3.0 * root * 0.044715) * square)
            gup = (slope * dot_nt(grad[run, :], down_here)).astype(BF16)
            act_s[run, :] = act
            gup_s[run, :] = gup
            grad_bias = grad_bias + jnp.sum(gup.astype(F32), axis=0, keepdims=True)
            total[run, :] += dot_nn(act, down_here)
            gnorm[run, :] += dot_nt(gup, up_here)
        small_up[pl.ds(s, 1), :] = grad_bias
        tmp[0] = dot_tn(normed[...], gup_s[...]).astype(BF16)
        tmp[1] = dot_tn(act_s[...], grad[...]).astype(BF16)
        for e in range(8):
            at = pl.multiple_of((me ^ e) * 64, 64)
            target = send if e % 2 else keep
            target[e // 2, s, 0:64, :] = tmp[0, pl.ds(at, 64), :]
            target[e // 2, s, 64:128, :] = tmp[1, pl.ds(at, 64), :]
        return carry

    lax.fori_loop(0, 4, hidden, 0)
    sums = [jnp.zeros((1, D), F32) for _ in range(4)]
    for start in range(0, ROWS, 256):
        run = slice(start, start + 256)
        middle = mid[run, :]
        out = (middle + (total[run, :] + b_down[...])).astype(BF16)
        if start < L1_ROW:
            y_quad[run, :] = out
        else:
            y_low[...] = out
        hat, rstd = moments(middle)
        back = gnorm[run, :]
        scaled = back * gain[...]
        cot = grad[run, :].astype(F32)
        mean_one = jnp.mean(scaled, axis=-1, keepdims=True)
        mean_two = jnp.mean(scaled * hat, axis=-1, keepdims=True)
        result = cot + rstd * (scaled - mean_one - hat * mean_two)
        gmid[run, :] = result
        terms = (cot, back * hat, back, result.astype(BF16).astype(F32))
        sums = [running + jnp.sum(term, axis=0, keepdims=True) for running, term in zip(sums, terms)]
    small[...] = jnp.concatenate(sums + [jnp.zeros((4, D), F32)], axis=0)


REVERSE = (0, 2, 1)


def attention_backward(scal, gmid, x_in, n_in, qkv, prob, ctx, w_full, gain, *rest):
    g_quad, g_low, keep, send, small = rest[:5]
    qx, kx, vx, cx, px, sx, heads_in, heads_out, attn, packed, tmp = rest[5:]
    me, live_steps = scal[0], scal[1]
    heads_in[...] = head_sum_matrix()
    heads_out[...] = head_spread_matrix()
    scale = 1.0 / math.sqrt(DH)
    for start in range(0, ROWS, 256):
        run = slice(start, start + 256)
        attn[run, :] = gmid[run, :].astype(BF16)
    tmp[3] = dot_tn(ctx[...], attn[...]).astype(BF16)

    def context_rows(at, count):
        row = lax.broadcasted_iota(jnp.int32, (count, 1), 0)
        step = row
        for start in (BLK, 2 * BLK, 3 * BLK):
            if start < count:
                step = jnp.where(row >= start, row - start, step)
        rows = dot_nt(attn[at : at + count, :], w_full[3]).astype(BF16).astype(F32)
        return jnp.where(step < live_steps, rows, 0.0)

    extend(qx, lambda at, count: qkv[0, at : at + count, :].astype(F32) * scale)
    extend(kx, lambda at, count: qkv[1, at : at + count, :].astype(F32))
    extend(vx, lambda at, count: qkv[2, at : at + count, :].astype(F32))
    extend(cx, context_rows)
    extend(px, lambda at, count: prob[at : at + count, :])
    packed[:, USED:ROWS, :] = jnp.zeros((3, ROWS - USED, D), BF16)
    scores = []
    for group, values, grads in zip(groups(kx), groups(vx), groups(cx)):
        first, count, level, child, keys = group
        slots = [s for s in range(len(keys)) if keys[s] is not None]
        cot = grads[4][0]()
        gprob = jnp.zeros((count, 128), F32)
        for s in slots:
            gprob = gprob + dot_nn((cot * values[4][s]()).astype(BF16), heads_in[D * s : D * s + D, :])
        here = prob[first : first + count, :]
        gscore = here * (gprob - slot_sum(here * gprob))
        tmp_rows = gscore.astype(BF16)
        gquery = jnp.zeros((count, D), F32)
        for s in slots:
            gquery = gquery + dot_nn(tmp_rows, heads_out[:, D * s : D * s + D]) * keys[s]()
        packed[0, first : first + count, :] = (gquery * scale).astype(BF16)
        scores.append((first, gscore))
    held = dict(scores)

    def score_rows(at, count):
        first = min(at // QUAD * QUAD, L2_ROW)
        return held[first][at - first : at - first + count, :]

    extend(sx, score_rows)
    for quers, grads, probs, scors in zip(groups(qx), groups(cx), groups(px), groups(sx)):
        first, count, level, child, queries = quers
        gkey = jnp.zeros((count, D), F32)
        gvalue = jnp.zeros((count, D), F32)
        for s in range(len(queries)):
            if queries[s] is None:
                continue
            weight, score = probs[4][s](), scors[4][s]()
            if s < 3:
                back = REVERSE[s]
            elif s == 3:
                back = 4 + child
            else:
                back = 3
            if level == 1 and s == 3:
                wide_p = jnp.concatenate(
                    [dot_nn(weight[0:BLK, :], heads_out[:, D * (4 + d) : D * (5 + d)]) for d in range(4)], axis=0
                )
                wide_s = jnp.concatenate(
                    [dot_nn(score[0:BLK, :], heads_out[:, D * (4 + d) : D * (5 + d)]) for d in range(4)], axis=0
                )
            else:
                wide_p = dot_nn(weight, heads_out[:, D * back : D * back + D])
                wide_s = dot_nn(score, heads_out[:, D * back : D * back + D])
            gkey = gkey + wide_s * queries[s]()
            gvalue = gvalue + wide_p * grads[4][s]()
        packed[1, first : first + count, :] = gkey.astype(BF16)
        packed[2, first : first + count, :] = gvalue.astype(BF16)
    for i in range(3):
        tmp[i] = dot_tn(n_in[...], packed[i]).astype(BF16)
    for e in range(8):
        piece = me ^ e
        at = pl.multiple_of(piece * 64, 64)
        target = send if e % 2 else keep
        for s in range(4):
            for i in range(3):
                target[e // 2, s, i] = tmp[i, pl.ds(at, 64), 128 * s : 128 * s + 128]
            top = pl.multiple_of(128 * s + 64 * (piece % 2), 64)
            side = pl.multiple_of(128 * (piece // 2), 128)
            target[e // 2, s, 3] = tmp[3, pl.ds(top, 64), pl.ds(side, 128)]
    sums = [jnp.zeros((1, D), F32) for _ in range(2)]
    for start in range(0, ROWS, 256):
        run = slice(start, start + 256)
        back = dot_nt(packed[0, run, :], w_full[0])
        back = back + dot_nt(packed[1, run, :], w_full[1])
        back = back + dot_nt(packed[2, run, :], w_full[2])
        hat, rstd = moments(x_in[run, :].astype(F32))
        scaled = back * gain[...]
        mean_one = jnp.mean(scaled, axis=-1, keepdims=True)
        mean_two = jnp.mean(scaled * hat, axis=-1, keepdims=True)
        result = (gmid[run, :] + rstd * (scaled - mean_one - hat * mean_two)).astype(BF16)
        if start < L1_ROW:
            g_quad[run, :] = result
        else:
            g_low[...] = result
        terms = (back * hat, back)
        sums = [running + jnp.sum(term, axis=0, keepdims=True) for running, term in zip(sums, terms)]
    small[...] = jnp.concatenate(sums + [jnp.zeros((6, D), F32)], axis=0)


def spread_rows(source, quad, low, recv, low0, low1, low2, out):
    moved = recv[...] + jnp.concatenate([low0[...], low1[...], low2[...], jnp.zeros((48, D), BF16)], axis=0)
    for start in range(0, SHARD, 240):
        run = slice(start, start + 240)
        rows = dot_nn(one_hot(source[run, :], 0, L1_ROW), quad[...])
        rows = rows + dot_nn(one_hot(source[run, :], L1_ROW, 256), low[...])
        rows = rows + dot_nn(one_hot(source[run, :], ROWS, L1_ROW), moved)
        out[run, :] = rows.astype(out.dtype)


def unpack_weights(scal, *rest):
    ins_a, ins_b = rest[:8], rest[8:16]
    g_qkv, g_out, g_up, g_down = rest[16:]
    me = scal[0]
    for e in range(8):
        piece = me ^ e
        at = pl.multiple_of(piece * 64, 64)
        g_up[pl.ds(at, 64), :] = ins_b[e][0:64, :].astype(F32)
        g_down[pl.ds(at, 64), :] = ins_b[e][64:128, :].astype(F32)
        for i in range(3):
            g_qkv[i, pl.ds(at, 64), :] = ins_a[e][i].astype(F32)
        top = pl.multiple_of(64 * (piece % 2), 64)
        side = pl.multiple_of(128 * (piece // 2), 128)
        g_out[pl.ds(top, 64), pl.ds(side, 128)] = ins_a[e][3].astype(F32)


def call(body, name, ins, outs, scratch=(), flops=0):
    specs = [pl.BlockSpec(memory_space=pltpu.VMEM)] * len(ins)
    if ins[0].ndim == 1:
        specs[0] = pl.BlockSpec(memory_space=pltpu.SMEM)
    size = sum(math.prod(v.shape) * v.dtype.itemsize for v in list(ins) + list(outs))
    return pl.pallas_call(
        body,
        out_shape=tuple(outs),
        in_specs=specs,
        out_specs=tuple(pl.BlockSpec(memory_space=pltpu.VMEM) for _ in outs),
        scratch_shapes=list(scratch),
        compiler_params=pltpu.CompilerParams(vmem_limit_bytes=VMEM_BYTES),
        cost_estimate=pl.CostEstimate(flops=flops, bytes_accessed=size, transcendentals=0),
        name=name,
    )(*ins)


def struct(shape, dtype):
    return jax.ShapeDtypeStruct(shape, dtype)


def shards(
    tokens,
    cotangent,
    lengths,
    neighbours,
    ln1_gain,
    ln1_shift,
    w_qkv,
    w_out,
    b_out,
    ln2_gain,
    ln2_shift,
    w_up,
    b_up,
    w_down,
    b_down,
    n_dp,
):
    j = lax.axis_index("dp")
    t = lax.axis_index("tensor")
    sub = j % 8

    def to_peer(value, e):
        return lax.ppermute(value, "dp", [(i, i ^ e) for i in range(n_dp)])

    def along(value, step):
        return lax.ppermute(value, "tensor", [(i, (i + step) % 4) for i in range(4)])

    def hop(value, pairs):
        return lax.ppermute(value, "tensor", pairs)

    def row(vec):
        return vec.reshape(1, -1)

    scal = jnp.stack([sub, lax.dynamic_index_in_dim(lengths, t, keepdims=False) // 16]).astype(jnp.int32)

    piece_a = jnp.concatenate(
        [
            lax.dynamic_slice(w_qkv, (0, 64 * sub, 0), (3, 64, 128)),
            lax.dynamic_slice(w_out, (64 * (sub % 2), 128 * (sub // 2)), (64, 128))[None],
        ],
        axis=0,
    )
    piece_b = jnp.concatenate(
        [
            lax.dynamic_slice(w_up, (64 * sub, 0), (64, D)),
            lax.dynamic_slice(w_down, (64 * sub, 0), (64, D)),
            row(b_up),
            jnp.zeros((15, D), BF16),
        ],
        axis=0,
    )

    def collect(piece):
        mine = jnp.stack([along(piece, s) for s in (1, 2, 3)])
        plane = [mine] + [to_peer(mine, e) for e in (2, 4, 6)]
        core = [to_peer(v, 1) for v in plane]
        return [v for pair in zip(plane, core) for v in pair]

    def bring(rows):
        tail = hop(rows[SEND_LO:], [(0, 1), (1, 2), (2, 3)])
        lows = []
        for w in range(3):
            part = jnp.concatenate(
                [rows[LOW_HEAD[w] : LOW_HEAD[w] + 192], rows[LOW_TAIL[w] : LOW_TAIL[w] + 64]], axis=0
            )
            lows.append(hop(part, [(3, w)]))
        return [rows, tail] + lows

    def give(quad, low, dtype):
        moved = hop(quad, [(1, 0), (2, 1), (3, 2)])
        lows = [hop(low[:240], [(w, 3)]) for w in range(3)]
        table = lax.dynamic_index_in_dim(jnp.asarray(spread_table()), t, keepdims=False)
        return call(
            spread_rows, "spread_rows", [table, quad, low, moved] + lows, [struct((SHARD, D), dtype)], flops=2 * SHARD * D * 1792
        )[0]

    pieces_a = collect(piece_a)
    own_rows = bring(tokens)
    source = lax.dynamic_index_in_dim(jnp.asarray(gather_table()), t, keepdims=False)
    act = struct((ROWS, D), BF16)
    x, n_one, qkv, prob, ctx, mid, w_full = call(
        attention_forward,
        "attention_forward",
        [scal, source] + own_rows + [row(ln1_gain), row(ln1_shift), row(b_out), w_qkv, w_out] + pieces_a,
        [
            act,
            act,
            struct((3, ROWS, D), BF16),
            struct((ROWS, 128), F32),
            act,
            struct((ROWS, D), F32),
            struct((4, D, D), BF16),
        ],
        [
            pltpu.VMEM((EXT, D), F32),
            pltpu.VMEM((EXT, D), F32),
            pltpu.VMEM((8 * D, 128), BF16),
            pltpu.VMEM((128, 8 * D), BF16),
        ],
        flops=2 * ROWS * D * 5000,
    )
    pieces_b = collect(piece_b)
    own_grads = bring(cotangent)
    half_b = struct((4, 4, 128, D), BF16)
    y_quad, y_low, keep_b, send_b, gmid, small_two, small_up = call(
        feed_forward,
        "feed_forward",
        [scal, source]
        + own_grads
        + [mid, row(ln2_gain), row(ln2_shift), row(b_down), w_up, row(b_up), w_down]
        + pieces_b,
        [
            struct((L1_ROW, D), BF16),
            struct((256, D), BF16),
            half_b,
            half_b,
            struct((ROWS, D), F32),
            struct((8, D), F32),
            struct((4, D), F32),
        ],
        [
            pltpu.VMEM((4, D, D), BF16),
            pltpu.VMEM((4, D, D), BF16),
            pltpu.VMEM((4, D), F32),
            pltpu.VMEM((ROWS, D), BF16),
            pltpu.VMEM((ROWS, D), BF16),
            pltpu.VMEM((ROWS, D), BF16),
            pltpu.VMEM((ROWS, D), BF16),
            pltpu.VMEM((ROWS, D), F32),
            pltpu.VMEM((ROWS, D), F32),
            pltpu.VMEM((2, D, D), BF16),
        ],
        flops=2 * ROWS * D * 14000,
    )
    output = give(y_quad, y_low, BF16)

    def lower(terms):
        return sum(v.astype(F32) for v in terms).astype(BF16)

    def reduce_weights(keep, send):
        both = lower([keep, to_peer(send, 1)])
        plane = lower([both[0]] + [to_peer(both[i], 2 * i) for i in (1, 2, 3)])
        bit = 8
        while bit < n_dp:
            plane = lower([plane, to_peer(plane, bit)])
            bit *= 2
        mine = lower([plane[0]] + [along(plane[s], -s) for s in (1, 2, 3)])
        flat = [mine] + [to_peer(mine, e) for e in (2, 4, 6)]
        core = [to_peer(v, 1) for v in flat]
        return [v for pair in zip(flat, core) for v in pair]

    sums_b = reduce_weights(keep_b, send_b)
    half_a = struct((4, 4, 4, 64, 128), BF16)
    g_quad, g_low, keep_a, send_a, small_one = call(
        attention_backward,
        "attention_backward",
        [scal, gmid, x, n_one, qkv, prob, ctx, w_full, row(ln1_gain)],
        [struct((L1_ROW, D), BF16), struct((256, D), BF16), half_a, half_a, struct((8, D), F32)],
        [
            pltpu.VMEM((EXT, D), F32),
            pltpu.VMEM((EXT, D), F32),
            pltpu.VMEM((EXT, D), F32),
            pltpu.VMEM((EXT, D), F32),
            pltpu.VMEM((EXT, 128), BF16),
            pltpu.VMEM((EXT, 128), BF16),
            pltpu.VMEM((8 * D, 128), BF16),
            pltpu.VMEM((128, 8 * D), BF16),
            pltpu.VMEM((ROWS, D), BF16),
            pltpu.VMEM((3, ROWS, D), BF16),
            pltpu.VMEM((4, D, D), BF16),
        ],
        flops=2 * ROWS * D * 9000,
    )
    sums_a = reduce_weights(keep_a, send_a)
    grad_tokens = give(g_quad, g_low, F32)
    g_qkv, g_out, g_up, g_down = call(
        unpack_weights,
        "unpack_weights",
        [scal] + sums_a + sums_b,
        [struct((3, D, 128), F32), struct((128, D), F32), struct((D, D), F32), struct((D, D), F32)],
    )
    up_rows = jnp.stack([lax.dynamic_index_in_dim(small_up, (t - a) % 4, keepdims=False) for a in range(4)])
    small = jnp.concatenate([small_two[:4], small_one[:2], jnp.zeros((2, D), F32), up_rows, jnp.zeros((4, D), F32)])
    bit = 1
    while bit < n_dp:
        small = small + to_peer(small, bit)
        bit *= 2
    small = small + along(small, 1) + along(small, 2) + along(small, 3)
    grad_b_up = lax.dynamic_index_in_dim(small, 8 + t, keepdims=False)
    return (
        output,
        grad_tokens,
        small[4],
        small[5],
        g_qkv,
        g_out,
        small[3],
        small[1],
        small[2],
        g_up,
        grad_b_up,
        g_down,
        small[0],
    )


def solution(mesh):
    n_dp = mesh.shape["dp"]
    placed = (
        P(("dp", "tensor"), None),
        P(("dp", "tensor"), None),
        P("dp"),
        P("dp", None),
        P(),
        P(),
        P(None, None, "tensor"),
        P("tensor", None),
        P(),
        P(),
        P(),
        P(None, "tensor"),
        P("tensor"),
        P("tensor", None),
        P(),
    )

    def run(*args):
        return shards(*args, n_dp)

    return jax.shard_map(
        run,
        mesh=mesh,
        in_specs=placed,
        out_specs=(
            P(("dp", "tensor"), None),
            P(("dp", "tensor"), None),
            P(),
            P(),
            P(None, None, "tensor"),
            P("tensor", None),
            P(),
            P(),
            P(),
            P(None, "tensor"),
            P("tensor"),
            P("tensor", None),
            P(),
        ),
        check_vma=False,
    )
```

```python
import math

import jax
import jax.numpy as jnp
from jax import lax
from jax.experimental import pallas as pl
from jax.experimental.pallas import tpu as pltpu
from jax.sharding import PartitionSpec as P

D = 512
DH = 64
MAXLEN = 720
NODES_GRP = 3840
SHARD = NODES_GRP // 4
F32 = jnp.float32
BF16 = jnp.bfloat16

BLK = 48
QUAD = 4 * BLK
L1_ROW = 4 * QUAD
L2_ROW = L1_ROW + QUAD
USED = L2_ROW + BLK
ROWS = 1024
EXT_C = (0, 240, 432, 672)
EXT_LEFT = (624, 0, 240, 432)
EXT_RIGHT = (240, 432, 672, 48)
EXT_L1 = 912
EXT_L2 = 1200
EXT = 1296
VMEM_BYTES = 60 * 1024 * 1024
SEND_LO = SHARD - MAXLEN
LOW_HEAD = (0, 176, 352)
LOW_TAIL = (720, 752, 800)


def split_blocks(row):
    block = row * 1366 >> 16
    return block, row - BLK * block


def gather_source(start, t):
    row = lax.broadcasted_iota(jnp.int32, (256, 1), 0) + start
    block, step = split_blocks(row)
    child, node = block >> 2, block & 3
    at = 720 - 240 * t + 16 * step + 4 * node + child
    level0 = jnp.where(at < 720, SHARD + at, at - 720)
    level1 = 4 * step + node + jnp.where(t == 3, 540, SHARD + 720 + 4 * t)
    tail = jnp.where(t == 0, 0, jnp.where(t == 1, 13, 10))
    level2 = step + jnp.where(t == 3, 855, SHARD + 720 + 192 + tail)
    spare = 3 * block + step - 45
    spare = jnp.where((t == 3) & (spare < 60) & (row < USED), 900 + spare, -1)
    live = jnp.where(row < L1_ROW, level0, jnp.where(row < L2_ROW, level1, level2))
    return jnp.where((step < 45) & (row < USED), live, spare)


def spread_source(start, t):
    row = lax.broadcasted_iota(jnp.int32, (240, 1), 0) + start
    at = 240 * t + row
    place = jnp.where(at < 720, at, at - 720)
    high = QUAD * (place & 3) + BLK * (place >> 2 & 3) + (place >> 4) + jnp.where(at < 720, 0, ROWS)
    first = (row >= 180).astype(jnp.int32) + (row >= 360).astype(jnp.int32) + (row >= 540).astype(jnp.int32)
    inside = row - 180 * first
    level1 = L1_ROW + BLK * (inside & 3) + (inside >> 2)
    rest = row - 720
    second = (rest >= 45).astype(jnp.int32) + (rest >= 90).astype(jnp.int32) + (rest >= 135).astype(jnp.int32)
    level2 = L2_ROW + rest - 45 * second
    spare = row - 900
    third = spare * 21846 >> 16
    low = jnp.where(row < 720, level1, level2)
    window = jnp.where(row < 720, first, second)
    low = jnp.where(window == 3, low, ROWS - L1_ROW + 240 * window + low)
    low = jnp.where(row < 900, low, BLK * third + 45 + spare - 3 * third)
    return jnp.where(t == 3, low, high)


def dot_nn(a, b):
    return jnp.dot(a, b, preferred_element_type=F32)


def dot_nt(a, b):
    return lax.dot_general(a, b, (((1,), (1,)), ((), ())), preferred_element_type=F32)


def dot_tn(a, b):
    return lax.dot_general(a, b, (((0,), (0,)), ((), ())), preferred_element_type=F32)


def one_hot(source, base, count):
    return (source - base == lax.broadcasted_iota(jnp.int32, (source.shape[0], count), 1)).astype(BF16)


def gathered_rows(start, t, own, recv, low):
    source = gather_source(start, t)
    total = dot_nn(one_hot(source, 0, SHARD), own[...])
    if start < L1_ROW:
        return total + dot_nn(one_hot(source, SHARD, 720), recv[...])
    return total + dot_nn(one_hot(source, SHARD + 720, 256), low[0][...] + low[1][...] + low[2][...])


def begin(sems, *pairs):
    copies = [pltpu.make_async_copy(src, dst, sems.at[i]) for i, (src, dst) in enumerate(pairs)]
    for copy in copies:
        copy.start()
    return copies


def finish(copies):
    for copy in copies:
        copy.wait()


def moments(values):
    center = values - jnp.mean(values, axis=-1, keepdims=True)
    spread = jnp.mean(center * center, axis=-1, keepdims=True)
    rstd = lax.rsqrt(spread + 1e-05)
    return center * rstd, rstd


def head_sum_matrix():
    row = lax.broadcasted_iota(jnp.int32, (8 * D, 128), 0)
    col = lax.broadcasted_iota(jnp.int32, (8 * D, 128), 1)
    return (row // DH == col % 64).astype(BF16)


def head_spread_matrix():
    row = lax.broadcasted_iota(jnp.int32, (128, 8 * D), 0)
    col = lax.broadcasted_iota(jnp.int32, (128, 8 * D), 1)
    return (row == col // DH).astype(BF16)


def slot_max(values):
    for step in (8, 16, 32):
        values = jnp.maximum(values, pltpu.roll(values, step, 1))
    return values


def slot_sum(values):
    for step in (8, 16, 32):
        values = values + pltpu.roll(values, step, 1)
    return values


def shift_down(block):
    row = lax.broadcasted_iota(jnp.int32, block.shape, 0)
    return jnp.where(row == 0, 0.0, pltpu.roll(block, 1, 0))


def shift_up(block):
    row = lax.broadcasted_iota(jnp.int32, block.shape, 0)
    return jnp.where(row == BLK - 1, 0.0, pltpu.roll(block, BLK - 1, 0))


def extend(ext, rows):
    kind = ext.dtype
    for c in range(4):
        ext[EXT_C[c] : EXT_C[c] + QUAD, :] = rows(QUAD * c, QUAD).astype(kind)
    ext[EXT_L1 : EXT_L1 + QUAD, :] = rows(L1_ROW, QUAD).astype(kind)
    last = rows(L2_ROW, BLK)
    ext[EXT_L2 : EXT_L2 + BLK, :] = last.astype(kind)
    ext[192:240, :] = shift_up(rows(0, BLK)).astype(kind)
    ext[624:672, :] = shift_down(rows(3 * QUAD + 144, BLK)).astype(kind)
    ext[864:912, :] = shift_down(rows(L1_ROW + 144, BLK)).astype(kind)
    ext[1104:1152, :] = shift_up(rows(L1_ROW, BLK)).astype(kind)
    ext[1152:1200, :] = shift_down(last).astype(kind)
    ext[1248:1296, :] = shift_up(last).astype(kind)


def present(count, level, child, live_steps):
    row = lax.broadcasted_iota(jnp.int32, (count, 128), 0)
    slot = lax.broadcasted_iota(jnp.int32, (count, 128), 1) % 64 // 8
    step = row
    for start in (BLK, 2 * BLK, 3 * BLK):
        if start < count:
            step = jnp.where(row >= start, row - start, step)
    here = step < live_steps
    if level == 0:
        here = here & (slot < 4)
    if level == 2:
        here = here & (slot != 3)
    if level > 0 or child == 0:
        here = here & ((slot != 1) | (row > 0))
    if level > 0 or child == 3:
        here = here & ((slot != 2) | (row < count - BLK) | (step + 1 < live_steps))
    return here


def groups(ext):
    def quad(at):
        return lambda: ext[at : at + QUAD, :]

    def block(at):
        return lambda: ext[at : at + BLK, :]

    def tiled(at):
        return lambda: jnp.concatenate([ext[at : at + BLK, :]] * 4, axis=0)

    out = []
    for c in range(4):
        out.append((QUAD * c, QUAD, 0, c, [quad(EXT_C[c]), quad(EXT_LEFT[c]), quad(EXT_RIGHT[c]), quad(EXT_L1)]))
    out.append(
        (L1_ROW, QUAD, 1, 0, [quad(EXT_L1), quad(864), quad(960), tiled(EXT_L2)] + [quad(EXT_C[c]) for c in range(4)])
    )
    children = [block(EXT_L1 + BLK * d) for d in range(4)]
    out.append((L2_ROW, BLK, 2, 0, [block(EXT_L2), block(1152), block(1248), None] + children))
    return out


def attention_forward(
    lengths, own, recv, low0, low1, low2, gain, shift, b_out, w_qkv, w_out, plane, other, *rest
):
    x_hbm, n_hbm, qkv_hbm, prob_out, ctx_out, mid_out, w_hbm = rest[:7]
    x_out, n_out, qkv_out, w_full, own_qkv, own_out, near, far, kx, vx, heads_in, heads_out, in_sems, out_sems = rest[7:]
    me, t = lax.axis_index("dp") & 7, lax.axis_index("tensor")
    live_steps = lengths[t] >> 4
    loading = begin(in_sems, (w_qkv, own_qkv), (w_out, own_out), (plane, near), (other, far))
    for start in range(0, ROWS, 256):
        run = slice(start, start + 256)
        rows = gathered_rows(start, t, own, recv, (low0, low1, low2))
        x_out[run, :] = rows.astype(BF16)
        n_out[run, :] = (moments(rows)[0] * gain[...] + shift[...]).astype(BF16)
    heads_in[...] = head_sum_matrix()
    heads_out[...] = head_spread_matrix()
    finish(loading)
    for i in range(3):
        w_full[i, :, 0:128] = own_qkv[i]
    w_full[3, 0:128, :] = own_out[...]
    for half, pieces in enumerate((near, far)):
        for k in range(4):
            parity = (me & 1) ^ half
            at = pl.multiple_of((2 * k + parity) * 64, 64)
            for s in range(1, 4):
                for i in range(3):
                    w_full[i, pl.ds(at, 64), 128 * s : 128 * s + 128] = pieces[k, s - 1, i]
                top = pl.multiple_of(128 * s + 64 * parity, 64)
                w_full[3, pl.ds(top, 64), 128 * k : 128 * k + 128] = pieces[k, s - 1, 3]
    for i in range(3):
        for start in range(0, ROWS, 512):
            run = slice(start, start + 512)
            qkv_out[i, run, :] = dot_nn(n_out[run, :], w_full[i]).astype(BF16)
    storing = begin(out_sems, (x_out, x_hbm), (n_out, n_hbm), (qkv_out, qkv_hbm), (w_full, w_hbm))
    extend(kx, lambda at, count: qkv_out[1, at : at + count, :].astype(F32))
    extend(vx, lambda at, count: qkv_out[2, at : at + count, :].astype(F32))
    ctx_out[USED:ROWS, :] = jnp.zeros((ROWS - USED, D), BF16)
    prob_out[USED:ROWS, :] = jnp.zeros((ROWS - USED, 128), F32)
    for (first, count, level, child, keys), (_, _, _, _, values) in zip(groups(kx), groups(vx)):
        query = qkv_out[0, first : first + count, :] * jnp.bfloat16(1.0 / math.sqrt(DH))
        slots = [s for s in range(len(keys)) if keys[s] is not None]
        score = jnp.zeros((count, 128), F32)
        for s in slots:
            score = score + dot_nn(query * keys[s](), heads_in[D * s : D * s + D, :])
        here = present(count, level, child, live_steps)
        score = jnp.where(here, score, -1000000000.0)
        weight = jnp.where(here, jnp.exp(score - slot_max(score)), 0.0)
        prob = weight / jnp.maximum(slot_sum(weight), 1.0)
        prob_out[first : first + count, :] = prob
        prob_low = prob.astype(BF16)
        context = jnp.zeros((count, D), F32)
        for s in slots:
            context = context + dot_nn(prob_low, heads_out[:, D * s : D * s + D]) * values[s]()
        ctx_out[first : first + count, :] = context.astype(BF16)
    for start in range(0, ROWS, 512):
        run = slice(start, start + 512)
        mid_out[run, :] = x_out[run, :].astype(F32) + dot_nn(ctx_out[run, :], w_full[3]) + b_out[...]
    finish(storing)


def feed_forward(
    own, recv, low0, low1, low2, mid, gain, shift, b_down, w_up, b_up, w_down, pieces, *rest
):
    y_quad, y_low, keep_hbm, send_hbm, gnorm, grad_hbm, grad_bias = rest[:7]
    up_w, down_w, up_t, down_t, bias, normed, grad, normed_t, grad_t = rest[7:16]
    act_s, gup_s, total, tmp, arrived, keep, send, in_sems, out_sems = rest[16:]
    me, t = lax.axis_index("dp") & 7, lax.axis_index("tensor")
    loading = begin(in_sems, (w_up, up_w.at[0]), (w_down, down_w.at[0]), (pieces, arrived))
    for start in range(0, ROWS, 256):
        run = slice(start, start + 256)
        low = (moments(mid[run, :])[0] * gain[...] + shift[...]).astype(BF16)
        normed[run, :] = low
        normed_t[:, run] = low.T
        cot = gathered_rows(start, t, own, recv, (low0, low1, low2)).astype(BF16)
        grad[run, :] = cot
        grad_t[:, run] = cot.T
    total[...] = jnp.zeros_like(total)
    gnorm[...] = jnp.zeros_like(gnorm)
    finish(loading)
    storing = begin(out_sems.at[8:9], (grad, grad_hbm))
    bias[0:1, :] = b_up[...].astype(F32)
    for piece in range(8):
        for s in range(1, 4):
            up_w[s, 64 * piece : 64 * piece + 64, :] = arrived[piece, s - 1, 0:64, :]
            down_w[s, 64 * piece : 64 * piece + 64, :] = arrived[piece, s - 1, 64:128, :]
    for s in range(1, 4):
        bias[s : s + 1, :] = arrived[0, s - 1, 128:129, :].astype(F32)

    def hidden(s, carry):
        up_here, down_here = up_w[s], down_w[s]
        up_t[...] = up_here.T
        down_t[...] = down_here.T
        sums = jnp.zeros((1, D), F32)
        for start in range(0, ROWS, 256):
            run = slice(start, start + 256)
            pre = dot_nn(normed[run, :], up_here) + bias[pl.ds(s, 1), :]
            square = pre * pre
            root = math.sqrt(2.0 / math.pi)
            bent = jnp.tanh(pre * (root + (root * 0.044715) * square))
            half = 0.5 * pre
            act = (half + half * bent).astype(BF16)
            slope = (0.5 + 0.5 * bent) + half * (1.0 - bent * bent) * (root + (3.0 * root * 0.044715) * square)
            gup = (slope * dot_nn(grad[run, :], down_t[...])).astype(BF16)
            act_s[run, :] = act
            gup_s[run, :] = gup
            sums = sums + jnp.sum(gup.astype(F32), axis=0, keepdims=True)
            total[run, :] += dot_nn(act, down_here)
            gnorm[run, :] += dot_nn(gup, up_t[...])
        grad_bias[pl.ds(s, 1), :] = sums
        tmp[0] = dot_nn(normed_t[...], gup_s[...]).astype(BF16)
        tmp[1] = dot_nn(grad_t[...], act_s[...]).astype(BF16)
        slot = ((t - s) & 3) ^ t
        for half, target in enumerate((keep, send)):
            for k in range(4):
                at = pl.multiple_of((me ^ (2 * k + half)) * 64, 64)
                target[slot, k, 0:64, :] = tmp[0, pl.ds(at, 64), :]
                target[slot, k, 64:128, :] = tmp[1, pl.ds(at, 64), :]
        begin(out_sems.at[pl.ds(2 * s, 2)], (keep.at[slot], keep_hbm.at[slot]), (send.at[slot], send_hbm.at[slot]))
        return carry

    lax.fori_loop(0, 4, hidden, 0)
    for start in range(0, ROWS, 256):
        run = slice(start, start + 256)
        out = (mid[run, :] + (total[run, :] + b_down[...])).astype(BF16)
        if start < L1_ROW:
            y_quad[run, :] = out
        else:
            y_low[...] = out[0 : USED - L1_ROW, :]
    for s in range(4):
        pltpu.make_async_copy(keep.at[s], keep_hbm.at[s], out_sems.at[2 * s]).wait()
        pltpu.make_async_copy(send.at[s], send_hbm.at[s], out_sems.at[2 * s + 1]).wait()
    finish(storing)


def norm_backward(lengths, mid, gnorm, grad, gain, ctx, w_full, keep_hbm, far_hbm, *rest):
    gmid, gcontext, gw_out, small = rest[:4]
    both, (attn, w_here, ctx_here, keep, far, sems) = rest[4:8], rest[8:]
    live_steps = lengths[lax.axis_index("tensor")] >> 4
    loading = begin(sems, (w_full.at[3], w_here), (ctx, ctx_here), (keep_hbm, keep), (far_hbm, far))
    finish(loading[:1])
    sums = [jnp.zeros((1, D), F32) for _ in range(4)]
    for start in range(0, ROWS, 256):
        run = slice(start, start + 256)
        hat, rstd = moments(mid[run, :])
        back = gnorm[run, :]
        scaled = back * gain[...]
        cot = grad[run, :].astype(F32)
        mean_one = jnp.mean(scaled, axis=-1, keepdims=True)
        mean_two = jnp.mean(scaled * hat, axis=-1, keepdims=True)
        result = cot + rstd * (scaled - mean_one - hat * mean_two)
        gmid[run, :] = result
        low = result.astype(BF16)
        attn[run, :] = low
        step = lax.broadcasted_iota(jnp.int32, (256, 1), 0) + start
        step = split_blocks(step)[1]
        gcontext[run, :] = jnp.where(step < live_steps, dot_nt(low, w_here[...]), 0.0).astype(BF16)
        terms = (cot, back * hat, back, low.astype(F32))
        sums = [running + jnp.sum(term, axis=0, keepdims=True) for running, term in zip(sums, terms)]
    finish(loading[1:])
    gw_out[...] = dot_tn(ctx_here[...], attn[...]).astype(BF16)
    for k in range(4):
        for slot in range(4):
            both[k][slot] = (keep[slot, k].astype(F32) + far[slot, k].astype(F32)).astype(BF16)
    small[...] = jnp.concatenate(sums + [jnp.zeros((4, D), F32)], axis=0)


REVERSE = (0, 2, 1)


def attention_backward(qkv, prob, gcontext, gain, small, small_up, gmid, x_in, n_in, gw_out, w_full, *rest):
    g_quad, g_low, keep, send = rest[:4]
    fx, cx, px, sx, heads_in, heads_out, packed, tmp = rest[4:12]
    bx, middle, x_here, n_here, gw_here, w_here, scores, sems = rest[12:]
    me, t = lax.axis_index("dp") & 7, lax.axis_index("tensor")
    loading = begin(sems, (gmid, middle), (x_in, x_here), (n_in, n_here), (gw_out, gw_here), (w_full, w_here))
    heads_in[...] = head_sum_matrix()
    heads_out[...] = head_spread_matrix()
    scale = 1.0 / math.sqrt(DH)
    extend(fx, lambda at, count: qkv[1, at : at + count, :].astype(F32))
    extend(bx, lambda at, count: qkv[2, at : at + count, :].astype(F32))
    packed[:, USED:ROWS, :] = jnp.zeros((3, ROWS - USED, D), BF16)
    for (first, count, level, child, keys), (_, _, _, _, values) in zip(groups(fx), groups(bx)):
        run = slice(first, first + count)
        slots = [s for s in range(len(keys)) if keys[s] is not None]
        cot = gcontext[run, :]
        gprob = jnp.zeros((count, 128), F32)
        for s in slots:
            gprob = gprob + dot_nn(cot * values[s](), heads_in[D * s : D * s + D, :])
        here = prob[run, :]
        gscore = (here * (gprob - slot_sum(here * gprob))).astype(BF16)
        scores[run, :] = gscore.astype(F32)
        gquery = jnp.zeros((count, D), F32)
        for s in slots:
            gquery = gquery + dot_nn(gscore, heads_out[:, D * s : D * s + D]) * keys[s]()
        packed[0, run, :] = (gquery * scale).astype(BF16)
    extend(fx, lambda at, count: qkv[0, at : at + count, :].astype(F32) * scale)
    extend(cx, lambda at, count: gcontext[at : at + count, :].astype(F32))
    extend(px, lambda at, count: prob[at : at + count, :])
    extend(sx, lambda at, count: scores[at : at + count, :])
    for quers, grads, probs, scors in zip(groups(fx), groups(cx), groups(px), groups(sx)):
        first, count, level, child, queries = quers
        gkey = jnp.zeros((count, D), F32)
        gvalue = jnp.zeros((count, D), F32)
        for s in range(len(queries)):
            if queries[s] is None:
                continue
            weight, score = probs[4][s](), scors[4][s]()
            if s < 3:
                back = REVERSE[s]
            elif s == 3:
                back = 4 + child
            else:
                back = 3
            if level == 1 and s == 3:
                wide_p = jnp.concatenate(
                    [dot_nn(weight[0:BLK, :], heads_out[:, D * (4 + d) : D * (5 + d)]) for d in range(4)], axis=0
                )
                wide_s = jnp.concatenate(
                    [dot_nn(score[0:BLK, :], heads_out[:, D * (4 + d) : D * (5 + d)]) for d in range(4)], axis=0
                )
            else:
                wide_p = dot_nn(weight, heads_out[:, D * back : D * back + D])
                wide_s = dot_nn(score, heads_out[:, D * back : D * back + D])
            gkey = gkey + wide_s * queries[s]()
            gvalue = gvalue + wide_p * grads[4][s]()
        packed[1, first : first + count, :] = gkey.astype(BF16)
        packed[2, first : first + count, :] = gvalue.astype(BF16)
    finish(loading)
    normed_t = n_here[...].T
    for i in range(3):
        tmp[i] = dot_nn(normed_t, packed[i]).astype(BF16)
    sums = [jnp.zeros((1, D), F32) for _ in range(2)]
    for start in range(0, ROWS, 256):
        run = slice(start, start + 256)
        back = dot_nt(packed[0, run, :], w_here[0])
        back = back + dot_nt(packed[1, run, :], w_here[1])
        back = back + dot_nt(packed[2, run, :], w_here[2])
        hat, rstd = moments(x_here[run, :].astype(F32))
        scaled = back * gain[...]
        mean_one = jnp.mean(scaled, axis=-1, keepdims=True)
        mean_two = jnp.mean(scaled * hat, axis=-1, keepdims=True)
        result = (middle[run, :] + rstd * (scaled - mean_one - hat * mean_two)).astype(BF16)
        if start < L1_ROW:
            g_quad[run, :] = result
        else:
            g_low[...] = result[0 : USED - L1_ROW, :]
        terms = (back * hat, back)
        sums = [running + jnp.sum(term, axis=0, keepdims=True) for running, term in zip(sums, terms)]
    sums = [small[i : i + 1, :] for i in range(4)] + sums
    for s in range(4):
        slot = ((t - s) & 3) ^ t
        vectors = sums + [small_up[s : s + 1, :]]
        rows = [vector[:, 128 * i : 128 * i + 128] for vector in vectors for i in range(4)]
        rows = jnp.concatenate(rows + [jnp.zeros((4, 128), F32)], axis=0).astype(BF16)
        for half, target in enumerate((keep, send)):
            for k in range(4):
                parity = (me & 1) ^ half
                at = pl.multiple_of((2 * k + parity) * 64, 64)
                for i in range(3):
                    target[k, slot, 64 * i : 64 * i + 64, :] = tmp[i, pl.ds(at, 64), 128 * s : 128 * s + 128]
                top = pl.multiple_of(128 * s + 64 * parity, 64)
                target[k, slot, 192:256, :] = gw_here[pl.ds(top, 64), 128 * k : 128 * k + 128]
                target[k, slot, 256:288, :] = rows


def spread_rows(quad, low, recv, low0, low1, low2, out):
    t = lax.axis_index("tensor")
    moved = recv[...] + jnp.concatenate([low0[...], low1[...], low2[...], jnp.zeros((48, D), BF16)], axis=0)
    for start in range(0, SHARD, 240):
        source = spread_source(start, t)
        rows = dot_nn(one_hot(source, 0, L1_ROW), quad[...])
        rows = rows + dot_nn(one_hot(source, L1_ROW, USED - L1_ROW), low[...])
        rows = rows + dot_nn(one_hot(source, ROWS, L1_ROW), moved)
        out[start : start + 240, :] = rows.astype(out.dtype)


def unpack_weights(in_a, in_b, g_qkv, g_out, g_up, g_down, down_t):
    for p in range(8):
        g_up[64 * p : 64 * p + 64, :] = in_b[p, 0:64, :].astype(F32)
        down_t[64 * p : 64 * p + 64, :] = in_b[p, 64:128, :].astype(F32)
    g_down[...] = down_t[...].T
    for p in range(8):
        for i in range(3):
            g_qkv[i, 64 * p : 64 * p + 64, :] = in_a[p, 64 * i : 64 * i + 64, :].astype(F32)
        top, side = 64 * (p % 2), 128 * (p // 2)
        g_out[top : top + 64, side : side + 128] = in_a[p, 192:256, :].astype(F32)


def call(body, name, ins, outs, scratch=(), moved=1000, far_ins=(), far_outs=()):
    specs = [pl.BlockSpec(memory_space=pl.ANY if i in far_ins else pltpu.VMEM) for i in range(len(ins))]
    if ins[0].ndim == 1:
        specs[0] = pl.BlockSpec(memory_space=pltpu.SMEM)
    return pl.pallas_call(
        body,
        out_shape=tuple(outs),
        in_specs=specs,
        out_specs=tuple(pl.BlockSpec(memory_space=pl.ANY if i in far_outs else pltpu.VMEM) for i in range(len(outs))),
        scratch_shapes=list(scratch),
        compiler_params=pltpu.CompilerParams(vmem_limit_bytes=VMEM_BYTES),
        cost_estimate=pl.CostEstimate(flops=1000, bytes_accessed=moved, transcendentals=0),
        name=name,
    )(*ins)


def struct(shape, dtype):
    return jax.ShapeDtypeStruct(shape, dtype)


def shards(
    tokens,
    cotangent,
    lengths,
    neighbours,
    ln1_gain,
    ln1_shift,
    w_qkv,
    w_out,
    b_out,
    ln2_gain,
    ln2_shift,
    w_up,
    b_up,
    w_down,
    b_down,
    n_dp,
):
    sub = lax.axis_index("dp") & 7
    planes = [[8 * g + 2 * k + c for k in range(4)] for g in range(n_dp // 8) for c in range(2)]
    eights = [[8 * g + k for k in range(8)] for g in range(n_dp // 8)]

    def to_peer(value, e):
        return lax.ppermute(value, "dp", [(i, i ^ e) for i in range(n_dp)])

    def along(value, step):
        return lax.ppermute(value, "tensor", [(i, (i + step) % 4) for i in range(4)])

    def hop(value, pairs):
        return lax.ppermute(value, "tensor", pairs)

    def row(vec):
        return vec.reshape(1, -1)

    def after(values, *others):
        return lax.optimization_barrier((values, others))[0]

    def lower(terms):
        return sum(v.astype(F32) for v in terms).astype(BF16)

    act, wide = struct((ROWS, D), BF16), struct((ROWS, D), F32)
    quad_rows, low_rows = struct((L1_ROW, D), BF16), struct((USED - L1_ROW, D), BF16)
    extended, narrow = pltpu.VMEM((EXT, D), F32), pltpu.VMEM((EXT, 128), BF16)
    sum_heads, spread_heads = pltpu.VMEM((8 * D, 128), BF16), pltpu.VMEM((128, 8 * D), BF16)

    piece_a = jnp.concatenate(
        [
            lax.dynamic_slice(w_qkv, (0, 64 * sub, 0), (3, 64, 128)),
            lax.dynamic_slice(w_out, (64 * (sub % 2), 128 * (sub // 2)), (64, 128))[None],
        ],
        axis=0,
    )
    piece = jnp.concatenate(
        [
            lax.dynamic_slice(w_up, (64 * sub, 0), (64, D)),
            lax.dynamic_slice(w_down, (64 * sub, 0), (64, D)),
            row(b_up),
            jnp.zeros((15, D), BF16),
            piece_a.swapaxes(0, 1).reshape(64, D),
        ],
        axis=0,
    )
    arrived = [along(piece, s) for s in (1, 2, 3)]
    first_a = jnp.stack([v[144:].reshape(64, 4, 128).swapaxes(0, 1) for v in arrived])
    first_b = jnp.stack([v[:144] for v in arrived])
    plane_a = lax.all_gather(first_a, "dp", axis=0, axis_index_groups=planes)
    other_a = to_peer(plane_a, 1)
    pieces_b = lax.all_gather(first_b, "dp", axis=0, axis_index_groups=eights)

    def bring(rows, *others):
        cuts = [rows[SEND_LO:]]
        for w in range(3):
            cuts.append(jnp.concatenate([rows[at : at + size] for at, size in ((LOW_HEAD[w], 192), (LOW_TAIL[w], 64))]))
        cuts = after(cuts, *others)
        return [hop(cuts[0], [(0, 1), (1, 2), (2, 3)])] + [hop(cuts[1 + w], [(3, w)]) for w in range(3)]

    token_rows = bring(tokens, first_a)
    grad_rows = bring(cotangent, *token_rows)
    rows_low = pltpu.VMEM((ROWS, D), BF16)
    all_rows = pltpu.VMEM((3, ROWS, D), BF16)
    weights = pltpu.VMEM((4, D, D), BF16)
    piece_rows = pltpu.VMEM((4, 3, 4, 64, 128), BF16)
    low_extended = pltpu.VMEM((EXT, D), BF16)
    sems = pltpu.SemaphoreType.DMA
    x, n_one, qkv, prob, ctx, mid, w_full = call(
        attention_forward,
        "attention_forward",
        [lengths, tokens] + token_rows + [row(ln1_gain), row(ln1_shift), row(b_out), w_qkv, w_out, plane_a, other_a],
        [act, act, struct((3, ROWS, D), BF16), struct((ROWS, 128), F32), act, wide, struct((4, D, D), BF16)],
        [
            rows_low,
            rows_low,
            all_rows,
            weights,
            pltpu.VMEM((3, D, 128), BF16),
            pltpu.VMEM((128, D), BF16),
            piece_rows,
            piece_rows,
            low_extended,
            extended,
            sum_heads,
            spread_heads,
            sems((4,)),
            sems((4,)),
        ],
        far_ins=(9, 10, 11, 12),
        far_outs=(0, 1, 2, 6),
    )
    half_b = struct((4, 4, 128, D), BF16)
    square = pltpu.VMEM((D, D), BF16)
    turned = pltpu.VMEM((D, ROWS), BF16)
    y_quad, y_low, keep_b, send_b, gnorm, grad, small_up = call(
        feed_forward,
        "feed_forward",
        [cotangent]
        + grad_rows
        + [mid, row(ln2_gain), row(ln2_shift), row(b_down), w_up, row(b_up), w_down, pieces_b],
        [quad_rows, low_rows, half_b, half_b, wide, act, struct((4, D), F32)],
        [weights, weights, square, square, pltpu.VMEM((4, D), F32), rows_low, rows_low, turned, turned]
        + [rows_low, rows_low, pltpu.VMEM((ROWS, D), F32), pltpu.VMEM((2, D, D), BF16)]
        + [pltpu.VMEM((8, 3, 144, D), BF16), pltpu.VMEM((4, 4, 128, D), BF16), pltpu.VMEM((4, 4, 128, D), BF16)]
        + [sems((3,)), sems((9,))],
        far_ins=(9, 11, 12),
        far_outs=(2, 3, 5),
    )
    far_send = to_peer(send_b, 1)
    piece_b = struct((4, 128, D), BF16)
    quarters = pltpu.VMEM((4, 4, 128, D), BF16)
    gmid, gcontext, gw_out, small, *both_b = call(
        norm_backward,
        "norm_backward",
        [lengths, mid, gnorm, grad, row(ln2_gain), ctx, w_full, keep_b, far_send],
        [wide, act, struct((D, D), BF16), struct((8, D), F32)] + [piece_b] * 4,
        [rows_low, square, rows_low, quarters, quarters, sems((4,))],
        25000000,
        far_ins=(5, 6, 7, 8),
    )

    def across(value, bits):
        return lax.ppermute(value, "tensor", [(i, i ^ bits) for i in range(4)])

    def wider(plane):
        bit = 8
        while bit < n_dp:
            plane = [lower([v, to_peer(v, bit)]) for v in plane]
            bit *= 2
        return plane

    left = [(1, 0), (2, 1), (3, 2)]
    y_lows = [hop(y_low, [(w, 3)]) for w in range(3)]
    gcontext = after(gcontext, y_lows[0], y_lows[1])
    y_recv = hop(after(y_quad, gcontext, y_lows[0], y_lows[1]), left)
    half_a = struct((4, 4, 288, 128), BF16)
    g_quad, g_low, keep_a, send_a = call(
        attention_backward,
        "attention_backward",
        [qkv, prob, gcontext, row(ln1_gain), small, small_up, gmid, x, n_one, gw_out, w_full],
        [quad_rows, low_rows, half_a, half_a],
        [extended, extended, narrow, narrow, sum_heads, spread_heads, all_rows, pltpu.VMEM((3, D, D), BF16)]
        + [low_extended, pltpu.VMEM((ROWS, D), F32), rows_low, rows_low, square, weights]
        + [pltpu.VMEM((ROWS, 128), F32), sems((5,))],
        60000000,
        far_ins=(6, 7, 8, 9, 10),
    )
    parts_b = after([both_b[0]] + [to_peer(both_b[k], 2 * k) for k in (1, 2, 3)], keep_a)
    far_a = to_peer(after(send_a, y_recv, *y_lows, *parts_b), 1)
    plane_b = wider([lower([v[s] for v in parts_b]) for s in range(4)])
    far_b = [across(plane_b[s], s) for s in (1, 2, 3)]
    both_a = lower([keep_a, far_a])
    parts_a = lax.all_to_all(both_a, "dp", 0, 0, axis_index_groups=planes, tiled=True)
    g_lows = [hop(after(g_low, both_a), [(w, 3)]) for w in range(3)]
    g_recv = hop(after(g_quad, both_a), left)
    parts_a = after(parts_a, g_recv, *g_lows)
    mine_b = lower([plane_b[0]] + after(far_b, parts_a))
    plane_a = wider([lower([parts_a[i, s] for i in range(4)]) for s in range(4)])
    flat_b = lax.all_gather(mine_b, "dp", axis=0, axis_index_groups=eights)
    output = call(
        spread_rows, "spread_rows", [after(y_quad, both_a), y_low, y_recv] + y_lows, [struct((SHARD, D), BF16)]
    )[0]
    mine_a = lower([plane_a[0]] + [across(plane_a[s], s) for s in (1, 2, 3)])
    grad_tokens = call(
        spread_rows, "spread_rows", [after(g_quad, parts_a), g_low, g_recv] + g_lows, [struct((SHARD, D), F32)]
    )[0]
    mine_a = after(mine_a, output, grad_tokens, mine_b)
    flat_a = lax.all_gather(mine_a, "dp", axis=0, axis_index_groups=eights)
    g_qkv, g_out, g_up, g_down = call(
        unpack_weights,
        "unpack_weights",
        [flat_a, flat_b],
        [struct((3, D, 128), F32), struct((128, D), F32), struct((D, D), F32), struct((D, D), F32)],
        [pltpu.VMEM((D, D), F32)],
    )
    sums = mine_a[256:284].astype(F32).reshape(7, D)
    return (
        output,
        grad_tokens,
        sums[4],
        sums[5],
        g_qkv,
        g_out,
        sums[3],
        sums[1],
        sums[2],
        g_up,
        sums[6],
        g_down,
        sums[0],
    )


def solution(mesh):
    n_dp = mesh.shape["dp"]
    placed = (
        P(("dp", "tensor"), None),
        P(("dp", "tensor"), None),
        P("dp"),
        P("dp", None),
        P(),
        P(),
        P(None, None, "tensor"),
        P("tensor", None),
        P(),
        P(),
        P(),
        P(None, "tensor"),
        P("tensor"),
        P("tensor", None),
        P(),
    )

    def run(*args):
        return shards(*args, n_dp)

    return jax.shard_map(
        run,
        mesh=mesh,
        in_specs=placed,
        out_specs=(
            P(("dp", "tensor"), None),
            P(("dp", "tensor"), None),
            P(),
            P(),
            P(None, None, "tensor"),
            P("tensor", None),
            P(),
            P(),
            P(),
            P(None, "tensor"),
            P("tensor"),
            P("tensor", None),
            P(),
        ),
        check_vma=False,
    )
```

```python
import math

import jax
import jax.numpy as jnp
from jax import lax
from jax.experimental import pallas as pl
from jax.experimental.pallas import tpu as pltpu
from jax.sharding import PartitionSpec as P

D = 512
DH = 64
MAXLEN = 720
NODES_GRP = 3840
SHARD = NODES_GRP // 4
F32 = jnp.float32
BF16 = jnp.bfloat16

BLK = 48
QUAD = 4 * BLK
L1_ROW = 4 * QUAD
L2_ROW = L1_ROW + QUAD
USED = L2_ROW + BLK
ROWS = 1024
EXT_C = (0, 240, 432, 672)
EXT_LEFT = (624, 0, 240, 432)
EXT_RIGHT = (240, 432, 672, 48)
EXT_L1 = 912
EXT_L2 = 1200
EXT = 1296
VMEM_BYTES = 60 * 1024 * 1024
SEND_LO = SHARD - MAXLEN
LOW_HEAD = (0, 176, 352)
LOW_TAIL = (720, 752, 800)


def split_blocks(row):
    block = row * 1366 >> 16
    return block, row - BLK * block


def gather_source(start, t):
    row = lax.broadcasted_iota(jnp.int32, (256, 1), 0) + start
    block, step = split_blocks(row)
    child, node = block >> 2, block & 3
    at = 720 - 240 * t + 16 * step + 4 * node + child
    level0 = jnp.where(at < 720, SHARD + at, at - 720)
    level1 = 4 * step + node + jnp.where(t == 3, 540, SHARD + 720 + 4 * t)
    tail = jnp.where(t == 0, 0, jnp.where(t == 1, 13, 10))
    level2 = step + jnp.where(t == 3, 855, SHARD + 720 + 192 + tail)
    spare = 3 * block + step - 45
    spare = jnp.where((t == 3) & (spare < 60) & (row < USED), 900 + spare, -1)
    live = jnp.where(row < L1_ROW, level0, jnp.where(row < L2_ROW, level1, level2))
    return jnp.where((step < 45) & (row < USED), live, spare)


def spread_source(start, t):
    row = lax.broadcasted_iota(jnp.int32, (240, 1), 0) + start
    at = 240 * t + row
    place = jnp.where(at < 720, at, at - 720)
    high = QUAD * (place & 3) + BLK * (place >> 2 & 3) + (place >> 4) + jnp.where(at < 720, 0, ROWS)
    first = (row >= 180).astype(jnp.int32) + (row >= 360).astype(jnp.int32) + (row >= 540).astype(jnp.int32)
    inside = row - 180 * first
    level1 = L1_ROW + BLK * (inside & 3) + (inside >> 2)
    rest = row - 720
    second = (rest >= 45).astype(jnp.int32) + (rest >= 90).astype(jnp.int32) + (rest >= 135).astype(jnp.int32)
    level2 = L2_ROW + rest - 45 * second
    spare = row - 900
    third = spare * 21846 >> 16
    low = jnp.where(row < 720, level1, level2)
    window = jnp.where(row < 720, first, second)
    low = jnp.where(window == 3, low, ROWS - L1_ROW + 240 * window + low)
    low = jnp.where(row < 900, low, BLK * third + 45 + spare - 3 * third)
    return jnp.where(t == 3, low, high)


def dot_nn(a, b):
    return jnp.dot(a, b, preferred_element_type=F32)


def dot_nt(a, b):
    return lax.dot_general(a, b, (((1,), (1,)), ((), ())), preferred_element_type=F32)


def dot_tn(a, b):
    return lax.dot_general(a, b, (((0,), (0,)), ((), ())), preferred_element_type=F32)


def one_hot(source, base, count):
    return (source - base == lax.broadcasted_iota(jnp.int32, (source.shape[0], count), 1)).astype(BF16)


def gathered_rows(start, t, own, recv, low):
    source = gather_source(start, t)
    total = dot_nn(one_hot(source, 0, SHARD), own[...])
    if start < L1_ROW:
        return total + dot_nn(one_hot(source, SHARD, 720), recv[...])
    return total + dot_nn(one_hot(source, SHARD + 720, 256), low[0][...] + low[1][...] + low[2][...])


def begin(sems, *pairs):
    copies = [pltpu.make_async_copy(src, dst, sems.at[i]) for i, (src, dst) in enumerate(pairs)]
    for copy in copies:
        copy.start()
    return copies


def finish(copies):
    for copy in copies:
        copy.wait()


def moments(values):
    center = values - jnp.mean(values, axis=-1, keepdims=True)
    spread = jnp.mean(center * center, axis=-1, keepdims=True)
    rstd = lax.rsqrt(spread + 1e-05)
    return center * rstd, rstd


def head_sum_matrix():
    row = lax.broadcasted_iota(jnp.int32, (8 * D, 128), 0)
    col = lax.broadcasted_iota(jnp.int32, (8 * D, 128), 1)
    return (row // DH == col % 64).astype(BF16)


def head_spread_matrix():
    row = lax.broadcasted_iota(jnp.int32, (128, 8 * D), 0)
    col = lax.broadcasted_iota(jnp.int32, (128, 8 * D), 1)
    return (row == col // DH).astype(BF16)


def slot_max(values):
    for step in (8, 16, 32):
        values = jnp.maximum(values, pltpu.roll(values, step, 1))
    return values


def slot_sum(values):
    for step in (8, 16, 32):
        values = values + pltpu.roll(values, step, 1)
    return values


def shift_down(block):
    row = lax.broadcasted_iota(jnp.int32, block.shape, 0)
    return jnp.where(row == 0, 0.0, pltpu.roll(block, 1, 0))


def shift_up(block):
    row = lax.broadcasted_iota(jnp.int32, block.shape, 0)
    return jnp.where(row == BLK - 1, 0.0, pltpu.roll(block, BLK - 1, 0))


def extend(ext, rows):
    kind = ext.dtype
    for c in range(4):
        ext[EXT_C[c] : EXT_C[c] + QUAD, :] = rows(QUAD * c, QUAD).astype(kind)
    ext[EXT_L1 : EXT_L1 + QUAD, :] = rows(L1_ROW, QUAD).astype(kind)
    last = rows(L2_ROW, BLK)
    ext[EXT_L2 : EXT_L2 + BLK, :] = last.astype(kind)
    ext[192:240, :] = shift_up(rows(0, BLK)).astype(kind)
    ext[624:672, :] = shift_down(rows(3 * QUAD + 144, BLK)).astype(kind)
    ext[864:912, :] = shift_down(rows(L1_ROW + 144, BLK)).astype(kind)
    ext[1104:1152, :] = shift_up(rows(L1_ROW, BLK)).astype(kind)
    ext[1152:1200, :] = shift_down(last).astype(kind)
    ext[1248:1296, :] = shift_up(last).astype(kind)


def present(count, level, child, live_steps):
    row = lax.broadcasted_iota(jnp.int32, (count, 128), 0)
    slot = lax.broadcasted_iota(jnp.int32, (count, 128), 1) % 64 // 8
    step = row
    for start in (BLK, 2 * BLK, 3 * BLK):
        if start < count:
            step = jnp.where(row >= start, row - start, step)
    here = step < live_steps
    if level == 0:
        here = here & (slot < 4)
    if level == 2:
        here = here & (slot != 3)
    if level > 0 or child == 0:
        here = here & ((slot != 1) | (row > 0))
    if level > 0 or child == 3:
        here = here & ((slot != 2) | (row < count - BLK) | (step + 1 < live_steps))
    return here


def groups(ext):
    def quad(at):
        return lambda: ext[at : at + QUAD, :]

    def block(at):
        return lambda: ext[at : at + BLK, :]

    def tiled(at):
        return lambda: jnp.concatenate([ext[at : at + BLK, :]] * 4, axis=0)

    out = []
    for c in range(4):
        out.append((QUAD * c, QUAD, 0, c, [quad(EXT_C[c]), quad(EXT_LEFT[c]), quad(EXT_RIGHT[c]), quad(EXT_L1)]))
    out.append(
        (L1_ROW, QUAD, 1, 0, [quad(EXT_L1), quad(864), quad(960), tiled(EXT_L2)] + [quad(EXT_C[c]) for c in range(4)])
    )
    children = [block(EXT_L1 + BLK * d) for d in range(4)]
    out.append((L2_ROW, BLK, 2, 0, [block(EXT_L2), block(1152), block(1248), None] + children))
    return out


def attention_forward(
    lengths, own, recv, low0, low1, low2, gain, shift, b_out, w_qkv, w_out, plane, other, *rest
):
    x_hbm, n_hbm, qkv_hbm, prob_out, ctx_out, mid_out, w_hbm = rest[:7]
    x_out, n_out, qkv_out, w_full, own_qkv, own_out, near, far, kx, vx, heads_in, heads_out, in_sems, out_sems = rest[7:]
    me, t = lax.axis_index("dp") & 7, lax.axis_index("tensor")
    live_steps = lengths[t] >> 4
    loading = begin(in_sems, (w_qkv, own_qkv), (w_out, own_out), (plane, near), (other, far))
    for start in range(0, ROWS, 256):
        run = slice(start, start + 256)
        rows = gathered_rows(start, t, own, recv, (low0, low1, low2))
        x_out[run, :] = rows.astype(BF16)
        n_out[run, :] = (moments(rows)[0] * gain[...] + shift[...]).astype(BF16)
    heads_in[...] = head_sum_matrix()
    heads_out[...] = head_spread_matrix()
    finish(loading)
    for i in range(3):
        w_full[i, :, 0:128] = own_qkv[i]
    w_full[3, 0:128, :] = own_out[...]
    for half, pieces in enumerate((near, far)):
        for k in range(4):
            parity = (me & 1) ^ half
            at = pl.multiple_of((2 * k + parity) * 64, 64)
            for s in range(1, 4):
                for i in range(3):
                    w_full[i, pl.ds(at, 64), 128 * s : 128 * s + 128] = pieces[k, s - 1, i]
                top = pl.multiple_of(128 * s + 64 * parity, 64)
                w_full[3, pl.ds(top, 64), 128 * k : 128 * k + 128] = pieces[k, s - 1, 3]
    for i in range(3):
        for start in range(0, ROWS, 512):
            run = slice(start, start + 512)
            qkv_out[i, run, :] = dot_nn(n_out[run, :], w_full[i]).astype(BF16)
    storing = begin(out_sems, (x_out, x_hbm), (n_out, n_hbm), (qkv_out, qkv_hbm), (w_full, w_hbm))
    extend(kx, lambda at, count: qkv_out[1, at : at + count, :].astype(F32))
    extend(vx, lambda at, count: qkv_out[2, at : at + count, :].astype(F32))
    ctx_out[USED:ROWS, :] = jnp.zeros((ROWS - USED, D), BF16)
    prob_out[USED:ROWS, :] = jnp.zeros((ROWS - USED, 128), F32)
    for (first, count, level, child, keys), (_, _, _, _, values) in zip(groups(kx), groups(vx)):
        query = qkv_out[0, first : first + count, :] * jnp.bfloat16(1.0 / math.sqrt(DH))
        slots = [s for s in range(len(keys)) if keys[s] is not None]
        score = jnp.zeros((count, 128), F32)
        for s in slots:
            score = score + dot_nn(query * keys[s](), heads_in[D * s : D * s + D, :])
        here = present(count, level, child, live_steps)
        score = jnp.where(here, score, -1000000000.0)
        weight = jnp.where(here, jnp.exp(score - slot_max(score)), 0.0)
        prob = weight / jnp.maximum(slot_sum(weight), 1.0)
        prob_out[first : first + count, :] = prob
        prob_low = prob.astype(BF16)
        context = jnp.zeros((count, D), F32)
        for s in slots:
            context = context + dot_nn(prob_low, heads_out[:, D * s : D * s + D]) * values[s]()
        ctx_out[first : first + count, :] = context.astype(BF16)
    for start in range(0, ROWS, 512):
        run = slice(start, start + 512)
        mid_out[run, :] = x_out[run, :].astype(F32) + dot_nn(ctx_out[run, :], w_full[3]) + b_out[...]
    finish(storing)


def feed_forward(
    own, recv, low0, low1, low2, mid, gain, shift, b_down, w_up, b_up, w_down, pieces, *rest
):
    y_quad, y_low, keep_hbm, send_hbm, gnorm, grad_hbm, grad_bias = rest[:7]
    up_w, down_w, up_t, down_t, bias, normed, grad, normed_t, grad_t = rest[7:16]
    act_s, gup_s, total, tmp, arrived, keep, send, in_sems, out_sems = rest[16:]
    me, t = lax.axis_index("dp") & 7, lax.axis_index("tensor")
    loading = begin(in_sems, (w_up, up_w.at[0]), (w_down, down_w.at[0]), (pieces, arrived))
    for start in range(0, ROWS, 256):
        run = slice(start, start + 256)
        low = (moments(mid[run, :])[0] * gain[...] + shift[...]).astype(BF16)
        normed[run, :] = low
        normed_t[:, run] = low.T
        cot = gathered_rows(start, t, own, recv, (low0, low1, low2)).astype(BF16)
        grad[run, :] = cot
        grad_t[:, run] = cot.T
    finish(loading)
    storing = begin(out_sems.at[8:9], (grad, grad_hbm))
    bias[0:1, :] = b_up[...].astype(F32)
    for piece in range(8):
        for s in range(1, 4):
            up_w[s, 64 * piece : 64 * piece + 64, :] = arrived[piece, s - 1, 0:64, :]
            down_w[s, 64 * piece : 64 * piece + 64, :] = arrived[piece, s - 1, 64:128, :]
    for s in range(1, 4):
        bias[s : s + 1, :] = arrived[0, s - 1, 128:129, :].astype(F32)

    for s in range(4):
        up_here, down_here = up_w[s], down_w[s]
        up_t[...] = up_here.T
        down_t[...] = down_here.T
        sums = jnp.zeros((1, D), F32)
        for start in range(0, ROWS, 512):
            run = slice(start, start + 512)
            pre = dot_nn(normed[run, :], up_here) + bias[pl.ds(s, 1), :]
            square = pre * pre
            root = math.sqrt(2.0 / math.pi)
            bent = jnp.tanh(pre * (root + (root * 0.044715) * square))
            half = 0.5 * pre
            act = (half + half * bent).astype(BF16)
            slope = (0.5 + 0.5 * bent) + half * (1.0 - bent * bent) * (root + (3.0 * root * 0.044715) * square)
            gup = (slope * dot_nn(grad[run, :], down_t[...])).astype(BF16)
            act_s[run, :] = act
            gup_s[run, :] = gup
            sums = sums + jnp.sum(gup.astype(F32), axis=0, keepdims=True)
            if s == 0:
                total[run, :] = dot_nn(act, down_here)
                gnorm[run, :] = dot_nn(gup, up_t[...])
            else:
                total[run, :] += dot_nn(act, down_here)
                gnorm[run, :] += dot_nn(gup, up_t[...])
        grad_bias[pl.ds(s, 1), :] = sums
        tmp[0] = dot_nn(normed_t[...], gup_s[...]).astype(BF16)
        tmp[1] = dot_nn(grad_t[...], act_s[...]).astype(BF16)
        slot = (t - s) & 3
        for half, target in enumerate((keep, send)):
            for k in range(4):
                at = pl.multiple_of((me ^ (2 * k + half)) * 64, 64)
                target[slot, k, 0:64, :] = tmp[0, pl.ds(at, 64), :]
                target[slot, k, 64:128, :] = tmp[1, pl.ds(at, 64), :]
        begin(out_sems.at[pl.ds(2 * s, 2)], (keep.at[slot], keep_hbm.at[slot]), (send.at[slot], send_hbm.at[slot]))
    for start in range(0, ROWS, 256):
        run = slice(start, start + 256)
        out = (mid[run, :] + (total[run, :] + b_down[...])).astype(BF16)
        if start < L1_ROW:
            y_quad[run, :] = out
        else:
            y_low[...] = out
    for s in range(4):
        pltpu.make_async_copy(keep.at[s], keep_hbm.at[s], out_sems.at[2 * s]).wait()
        pltpu.make_async_copy(send.at[s], send_hbm.at[s], out_sems.at[2 * s + 1]).wait()
    finish(storing)


def norm_backward(lengths, mid, gnorm, grad, gain, ctx, w_full, *rest):
    gmid, gcontext, gw_out, small = rest[:4]
    attn, w_here, ctx_here, sems = rest[4:]
    live_steps = lengths[lax.axis_index("tensor")] >> 4
    loading = begin(sems, (w_full.at[3], w_here), (ctx, ctx_here))
    finish(loading[:1])
    sums = [jnp.zeros((1, D), F32) for _ in range(4)]
    for start in range(0, ROWS, 256):
        run = slice(start, start + 256)
        hat, rstd = moments(mid[run, :])
        back = gnorm[run, :]
        scaled = back * gain[...]
        cot = grad[run, :].astype(F32)
        mean_one = jnp.mean(scaled, axis=-1, keepdims=True)
        mean_two = jnp.mean(scaled * hat, axis=-1, keepdims=True)
        result = cot + rstd * (scaled - mean_one - hat * mean_two)
        gmid[run, :] = result
        low = result.astype(BF16)
        attn[run, :] = low
        step = lax.broadcasted_iota(jnp.int32, (256, 1), 0) + start
        step = split_blocks(step)[1]
        gcontext[run, :] = jnp.where(step < live_steps, dot_nt(low, w_here[...]), 0.0).astype(BF16)
        terms = (cot, back * hat, back, low.astype(F32))
        sums = [running + jnp.sum(term, axis=0, keepdims=True) for running, term in zip(sums, terms)]
    finish(loading[1:])
    gw_out[...] = dot_tn(ctx_here[...], attn[...]).astype(BF16)
    small[...] = jnp.concatenate(sums + [jnp.zeros((4, D), F32)], axis=0)


def pair_sum(keep, far, *both):
    for k in range(4):
        for slot in range(4):
            both[k][slot] = (keep[slot, k].astype(F32) + far[slot, k].astype(F32)).astype(BF16)


REVERSE = (0, 2, 1)


def attention_backward(qkv, prob, gcontext, gain, small, small_up, gmid, x_in, n_in, gw_out, w_full, *rest):
    g_quad, g_low, keep, send = rest[:4]
    fx, cx, px, sx, heads_in, heads_out, packed, tmp = rest[4:12]
    bx, middle, x_here, n_here, gw_here, w_here, scores, sems = rest[12:]
    me, t = lax.axis_index("dp") & 7, lax.axis_index("tensor")
    loading = begin(sems, (gmid, middle), (x_in, x_here), (n_in, n_here), (gw_out, gw_here), (w_full, w_here))
    heads_in[...] = head_sum_matrix()
    heads_out[...] = head_spread_matrix()
    scale = 1.0 / math.sqrt(DH)
    extend(fx, lambda at, count: qkv[1, at : at + count, :].astype(F32))
    extend(bx, lambda at, count: qkv[2, at : at + count, :].astype(F32))
    packed[:, USED:ROWS, :] = jnp.zeros((3, ROWS - USED, D), BF16)
    for (first, count, level, child, keys), (_, _, _, _, values) in zip(groups(fx), groups(bx)):
        run = slice(first, first + count)
        slots = [s for s in range(len(keys)) if keys[s] is not None]
        cot = gcontext[run, :]
        gprob = jnp.zeros((count, 128), F32)
        for s in slots:
            gprob = gprob + dot_nn(cot * values[s](), heads_in[D * s : D * s + D, :])
        here = prob[run, :]
        gscore = (here * (gprob - slot_sum(here * gprob))).astype(BF16)
        scores[run, :] = gscore.astype(F32)
        gquery = jnp.zeros((count, D), F32)
        for s in slots:
            gquery = gquery + dot_nn(gscore, heads_out[:, D * s : D * s + D]) * keys[s]()
        packed[0, run, :] = (gquery * scale).astype(BF16)
    extend(fx, lambda at, count: qkv[0, at : at + count, :].astype(F32) * scale)
    extend(cx, lambda at, count: gcontext[at : at + count, :].astype(F32))
    extend(px, lambda at, count: prob[at : at + count, :])
    extend(sx, lambda at, count: scores[at : at + count, :])
    for quers, grads, probs, scors in zip(groups(fx), groups(cx), groups(px), groups(sx)):
        first, count, level, child, queries = quers
        gkey = jnp.zeros((count, D), F32)
        gvalue = jnp.zeros((count, D), F32)
        for s in range(len(queries)):
            if queries[s] is None:
                continue
            weight, score = probs[4][s](), scors[4][s]()
            if s < 3:
                back = REVERSE[s]
            elif s == 3:
                back = 4 + child
            else:
                back = 3
            if level == 1 and s == 3:
                wide_p = jnp.concatenate(
                    [dot_nn(weight[0:BLK, :], heads_out[:, D * (4 + d) : D * (5 + d)]) for d in range(4)], axis=0
                )
                wide_s = jnp.concatenate(
                    [dot_nn(score[0:BLK, :], heads_out[:, D * (4 + d) : D * (5 + d)]) for d in range(4)], axis=0
                )
            else:
                wide_p = dot_nn(weight, heads_out[:, D * back : D * back + D])
                wide_s = dot_nn(score, heads_out[:, D * back : D * back + D])
            gkey = gkey + wide_s * queries[s]()
            gvalue = gvalue + wide_p * grads[4][s]()
        packed[1, first : first + count, :] = gkey.astype(BF16)
        packed[2, first : first + count, :] = gvalue.astype(BF16)
    finish(loading)
    normed_t = n_here[...].T
    for i in range(3):
        tmp[i] = dot_nn(normed_t, packed[i]).astype(BF16)
    sums = [jnp.zeros((1, D), F32) for _ in range(2)]
    for start in range(0, ROWS, 256):
        run = slice(start, start + 256)
        back = dot_nt(packed[0, run, :], w_here[0])
        back = back + dot_nt(packed[1, run, :], w_here[1])
        back = back + dot_nt(packed[2, run, :], w_here[2])
        hat, rstd = moments(x_here[run, :].astype(F32))
        scaled = back * gain[...]
        mean_one = jnp.mean(scaled, axis=-1, keepdims=True)
        mean_two = jnp.mean(scaled * hat, axis=-1, keepdims=True)
        result = (middle[run, :] + rstd * (scaled - mean_one - hat * mean_two)).astype(BF16)
        if start < L1_ROW:
            g_quad[run, :] = result
        else:
            g_low[...] = result[0 : USED - L1_ROW, :]
        terms = (back * hat, back)
        sums = [running + jnp.sum(term, axis=0, keepdims=True) for running, term in zip(sums, terms)]
    sums = [small[i : i + 1, :] for i in range(4)] + sums
    for s in range(4):
        slot = ((t - s) & 3) ^ t
        vectors = sums + [small_up[s : s + 1, :]]
        rows = [vector[:, 128 * i : 128 * i + 128] for vector in vectors for i in range(4)]
        rows = jnp.concatenate(rows + [jnp.zeros((4, 128), F32)], axis=0).astype(BF16)
        for half, target in enumerate((keep, send)):
            for k in range(4):
                parity = (me & 1) ^ half
                at = pl.multiple_of((2 * k + parity) * 64, 64)
                for i in range(3):
                    target[k, slot, 64 * i : 64 * i + 64, :] = tmp[i, pl.ds(at, 64), 128 * s : 128 * s + 128]
                top = pl.multiple_of(128 * s + 64 * parity, 64)
                target[k, slot, 192:256, :] = gw_here[pl.ds(top, 64), 128 * k : 128 * k + 128]
                target[k, slot, 256:288, :] = rows


def spread_rows(quad, low, recv, *rest):
    t, (*lows, out) = lax.axis_index("tensor"), rest
    count = USED - L1_ROW
    if len(lows) == 3:
        others = [part[...] for part in lows]
    else:
        others = [jnp.where(t == 3, lows[0][w, 0:count, :], jnp.zeros((count, D), BF16)) for w in range(3)]
    moved = recv[...] + jnp.concatenate(others + [jnp.zeros((48, D), BF16)], axis=0)
    for start in range(0, SHARD, 240):
        source = spread_source(start, t)
        rows = dot_nn(one_hot(source, 0, L1_ROW), quad[...])
        rows = rows + dot_nn(one_hot(source, L1_ROW, count), low[0:count, :])
        rows = rows + dot_nn(one_hot(source, ROWS, L1_ROW), moved)
        out[start : start + 240, :] = rows.astype(out.dtype)


def unpack_weights(in_a, in_b, g_qkv, g_out, g_up, g_down, down_t):
    for p in range(8):
        g_up[64 * p : 64 * p + 64, :] = in_b[p, 0:64, :].astype(F32)
        down_t[64 * p : 64 * p + 64, :] = in_b[p, 64:128, :].astype(F32)
    g_down[...] = down_t[...].T
    for p in range(8):
        for i in range(3):
            g_qkv[i, 64 * p : 64 * p + 64, :] = in_a[p, 64 * i : 64 * i + 64, :].astype(F32)
        top, side = 64 * (p % 2), 128 * (p // 2)
        g_out[top : top + 64, side : side + 128] = in_a[p, 192:256, :].astype(F32)


def call(body, name, ins, outs, scratch=(), moved=1000, far_ins=(), far_outs=()):
    specs = [pl.BlockSpec(memory_space=pl.ANY if i in far_ins else pltpu.VMEM) for i in range(len(ins))]
    if ins[0].ndim == 1:
        specs[0] = pl.BlockSpec(memory_space=pltpu.SMEM)
    return pl.pallas_call(
        body,
        out_shape=tuple(outs),
        in_specs=specs,
        out_specs=tuple(pl.BlockSpec(memory_space=pl.ANY if i in far_outs else pltpu.VMEM) for i in range(len(outs))),
        scratch_shapes=list(scratch),
        compiler_params=pltpu.CompilerParams(vmem_limit_bytes=VMEM_BYTES),
        cost_estimate=pl.CostEstimate(flops=1000, bytes_accessed=moved, transcendentals=0),
        name=name,
    )(*ins)


def struct(shape, dtype):
    return jax.ShapeDtypeStruct(shape, dtype)


def shards(
    tokens,
    cotangent,
    lengths,
    neighbours,
    ln1_gain,
    ln1_shift,
    w_qkv,
    w_out,
    b_out,
    ln2_gain,
    ln2_shift,
    w_up,
    b_up,
    w_down,
    b_down,
    n_dp,
):
    sub = lax.axis_index("dp") & 7
    planes = [[8 * g + 2 * k + c for k in range(4)] for g in range(n_dp // 8) for c in range(2)]
    eights = [[8 * g + k for k in range(8)] for g in range(n_dp // 8)]

    def to_peer(value, e):
        return lax.ppermute(value, "dp", [(i, i ^ e) for i in range(n_dp)])

    def along(value, step):
        return lax.ppermute(value, "tensor", [(i, (i + step) % 4) for i in range(4)])

    def hop(value, pairs):
        return lax.ppermute(value, "tensor", pairs)

    def row(vec):
        return vec.reshape(1, -1)

    def after(values, *others):
        return lax.optimization_barrier((values, others))[0]

    def lower(terms):
        return sum(v.astype(F32) for v in terms).astype(BF16)

    act, wide = struct((ROWS, D), BF16), struct((ROWS, D), F32)
    quad_rows, low_rows = struct((L1_ROW, D), BF16), struct((USED - L1_ROW, D), BF16)
    extended, narrow = pltpu.VMEM((EXT, D), F32), pltpu.VMEM((EXT, 128), BF16)
    sum_heads, spread_heads = pltpu.VMEM((8 * D, 128), BF16), pltpu.VMEM((128, 8 * D), BF16)

    piece_a = jnp.concatenate(
        [
            lax.dynamic_slice(w_qkv, (0, 64 * sub, 0), (3, 64, 128)),
            lax.dynamic_slice(w_out, (64 * (sub % 2), 128 * (sub // 2)), (64, 128))[None],
        ],
        axis=0,
    )
    piece = jnp.concatenate(
        [
            lax.dynamic_slice(w_up, (64 * sub, 0), (64, D)),
            lax.dynamic_slice(w_down, (64 * sub, 0), (64, D)),
            row(b_up),
            jnp.zeros((15, D), BF16),
            piece_a.swapaxes(0, 1).reshape(64, D),
        ],
        axis=0,
    )
    arrived = [along(piece, s) for s in (1, 2, 3)]
    first_a = jnp.stack([v[144:].reshape(64, 4, 128).swapaxes(0, 1) for v in arrived])
    first_b = jnp.stack([v[:144] for v in arrived])
    plane_a = lax.all_gather(first_a, "dp", axis=0, axis_index_groups=planes)
    other_a = to_peer(plane_a, 1)
    pieces_b = lax.all_gather(first_b, "dp", axis=0, axis_index_groups=eights)

    def bring(rows, *others):
        cuts = [rows[SEND_LO:]]
        for w in range(3):
            cuts.append(jnp.concatenate([rows[at : at + size] for at, size in ((LOW_HEAD[w], 192), (LOW_TAIL[w], 64))]))
        cuts = after(cuts, *others)
        return [hop(cuts[0], [(0, 1), (1, 2), (2, 3)])] + [hop(cuts[1 + w], [(3, w)]) for w in range(3)]

    token_rows = bring(tokens, first_a)
    grad_rows = bring(cotangent, *token_rows)
    rows_low = pltpu.VMEM((ROWS, D), BF16)
    all_rows = pltpu.VMEM((3, ROWS, D), BF16)
    weights = pltpu.VMEM((4, D, D), BF16)
    piece_rows = pltpu.VMEM((4, 3, 4, 64, 128), BF16)
    low_extended = pltpu.VMEM((EXT, D), BF16)
    sems = pltpu.SemaphoreType.DMA
    x, n_one, qkv, prob, ctx, mid, w_full = call(
        attention_forward,
        "attention_forward",
        [lengths, tokens] + token_rows + [row(ln1_gain), row(ln1_shift), row(b_out), w_qkv, w_out, plane_a, other_a],
        [act, act, struct((3, ROWS, D), BF16), struct((ROWS, 128), F32), act, wide, struct((4, D, D), BF16)],
        [
            rows_low,
            rows_low,
            all_rows,
            weights,
            pltpu.VMEM((3, D, 128), BF16),
            pltpu.VMEM((128, D), BF16),
            piece_rows,
            piece_rows,
            low_extended,
            extended,
            sum_heads,
            spread_heads,
            sems((4,)),
            sems((4,)),
        ],
        far_ins=(9, 10, 11, 12),
        far_outs=(0, 1, 2, 6),
    )
    half_b = struct((4, 4, 128, D), BF16)
    square = pltpu.VMEM((D, D), BF16)
    turned = pltpu.VMEM((D, ROWS), BF16)
    y_quad, y_low, keep_b, send_b, gnorm, grad, small_up = call(
        feed_forward,
        "feed_forward",
        [cotangent]
        + grad_rows
        + [mid, row(ln2_gain), row(ln2_shift), row(b_down), w_up, row(b_up), w_down, pieces_b],
        [quad_rows, struct((256, D), BF16), half_b, half_b, wide, act, struct((4, D), F32)],
        [weights, weights, square, square, pltpu.VMEM((4, D), F32), rows_low, rows_low, turned, turned]
        + [rows_low, rows_low, pltpu.VMEM((ROWS, D), F32), pltpu.VMEM((2, D, D), BF16)]
        + [pltpu.VMEM((8, 3, 144, D), BF16), pltpu.VMEM((4, 4, 128, D), BF16), pltpu.VMEM((4, 4, 128, D), BF16)]
        + [sems((3,)), sems((9,))],
        far_ins=(9, 11, 12),
        far_outs=(2, 3, 5),
    )
    far_send = to_peer(send_b, 1)
    gmid, gcontext, gw_out, small = call(
        norm_backward,
        "norm_backward",
        [lengths, mid, gnorm, grad, row(ln2_gain), ctx, w_full],
        [wide, act, struct((D, D), BF16), struct((8, D), F32)],
        [rows_low, square, rows_low, sems((2,))],
        25000000,
        far_ins=(5, 6),
    )
    both_b = call(pair_sum, "pair_sum", [keep_b, after(far_send, small)], [struct((4, 128, D), BF16)] * 4)

    def across(value, bits):
        return lax.ppermute(value, "tensor", [(i, i ^ bits) for i in range(4)])

    def wider(plane):
        bit = 8
        while bit < n_dp:
            plane = [lower([v, to_peer(v, bit)]) for v in plane]
            bit *= 2
        return plane

    left = [(1, 0), (2, 1), (3, 2)]
    y_lows = [lax.all_gather(y_low, "tensor", axis=0)]
    y_recv = hop(after(y_quad, gcontext), left)
    half_a = struct((4, 4, 288, 128), BF16)
    g_quad, g_low, keep_a, send_a = call(
        attention_backward,
        "attention_backward",
        [qkv, prob, gcontext, row(ln1_gain), small, small_up, gmid, x, n_one, gw_out, w_full],
        [quad_rows, low_rows, half_a, half_a],
        [extended, extended, narrow, narrow, sum_heads, spread_heads, all_rows, pltpu.VMEM((3, D, D), BF16)]
        + [low_extended, pltpu.VMEM((ROWS, D), F32), rows_low, rows_low, square, weights]
        + [pltpu.VMEM((ROWS, 128), F32), sems((5,))],
        60000000,
        far_ins=(6, 7, 8, 9, 10),
    )
    parts_b = after([both_b[0]] + [to_peer(both_b[k], 2 * k) for k in (1, 2, 3)], keep_a)
    far_a = to_peer(after(send_a, y_recv, *y_lows, *parts_b), 1)
    plane_b = wider([lower([v[s] for v in parts_b]) for s in range(4)])
    mine_b = lax.psum_scatter(jnp.concatenate(plane_b), "tensor", scatter_dimension=0, tiled=True)
    both_a = lower([keep_a, far_a])
    parts_a = lax.all_to_all(both_a, "dp", 0, 0, axis_index_groups=planes, tiled=True)
    g_lows = [hop(after(g_low, both_a), [(w, 3)]) for w in range(3)]
    g_recv = hop(after(g_quad, both_a), left)
    output = call(
        spread_rows, "spread_rows", [after(y_quad, both_a), y_low, y_recv] + y_lows, [struct((SHARD, D), BF16)]
    )[0]
    parts_a = after(parts_a, g_recv, output, *g_lows)
    plane_a = wider([lower([parts_a[i, s] for i in range(4)]) for s in range(4)])
    mine_b = after(mine_b, parts_a)
    flat_b = lax.all_gather(mine_b, "dp", axis=0, axis_index_groups=eights)
    mine_a = lower([plane_a[0]] + [across(plane_a[s], s) for s in (1, 2, 3)])
    grad_tokens = call(
        spread_rows, "spread_rows", [after(g_quad, parts_a), g_low, g_recv] + g_lows, [struct((SHARD, D), F32)]
    )[0]
    mine_a = after(mine_a, output, grad_tokens, mine_b)
    flat_a = lax.all_gather(mine_a, "dp", axis=0, axis_index_groups=eights)
    g_qkv, g_out, g_up, g_down = call(
        unpack_weights,
        "unpack_weights",
        [flat_a, flat_b],
        [struct((3, D, 128), F32), struct((128, D), F32), struct((D, D), F32), struct((D, D), F32)],
        [pltpu.VMEM((D, D), F32)],
    )
    sums = mine_a[256:284].astype(F32).reshape(7, D)
    return (
        output,
        grad_tokens,
        sums[4],
        sums[5],
        g_qkv,
        g_out,
        sums[3],
        sums[1],
        sums[2],
        g_up,
        sums[6],
        g_down,
        sums[0],
    )


def solution(mesh):
    n_dp = mesh.shape["dp"]
    placed = (
        P(("dp", "tensor"), None),
        P(("dp", "tensor"), None),
        P("dp"),
        P("dp", None),
        P(),
        P(),
        P(None, None, "tensor"),
        P("tensor", None),
        P(),
        P(),
        P(),
        P(None, "tensor"),
        P("tensor"),
        P("tensor", None),
        P(),
    )

    def run(*args):
        return shards(*args, n_dp)

    return jax.shard_map(
        run,
        mesh=mesh,
        in_specs=placed,
        out_specs=(
            P(("dp", "tensor"), None),
            P(("dp", "tensor"), None),
            P(),
            P(),
            P(None, None, "tensor"),
            P("tensor", None),
            P(),
            P(),
            P(),
            P(None, "tensor"),
            P("tensor"),
            P("tensor", None),
            P(),
        ),
        check_vma=False,
    )
```

```python
import math

import jax
import jax.numpy as jnp
from jax import lax
from jax.experimental import pallas as pl
from jax.experimental.pallas import tpu as pltpu
from jax.sharding import PartitionSpec as P

D = 512
DH = 64
MAXLEN = 720
NODES_GRP = 3840
SHARD = NODES_GRP // 4
F32 = jnp.float32
BF16 = jnp.bfloat16

BLK = 48
QUAD = 4 * BLK
L1_ROW = 4 * QUAD
L2_ROW = L1_ROW + QUAD
USED = L2_ROW + BLK
ROWS = 1024
EXT_C = (0, 240, 432, 672)
EXT_LEFT = (624, 0, 240, 432)
EXT_RIGHT = (240, 432, 672, 48)
EXT_L1 = 912
EXT_L2 = 1200
EXT = 1296
VMEM_BYTES = 60 * 1024 * 1024
SEND_LO = SHARD - MAXLEN
LOW_HEAD = (0, 176, 352)
LOW_TAIL = (720, 752, 800)


def split_blocks(row):
    block = row * 1366 >> 16
    return block, row - BLK * block


def gather_source(start, t):
    row = lax.broadcasted_iota(jnp.int32, (256, 1), 0) + start
    block, step = split_blocks(row)
    child, node = block >> 2, block & 3
    at = 720 - 240 * t + 16 * step + 4 * node + child
    level0 = jnp.where(at < 720, SHARD + at, at - 720)
    level1 = 4 * step + node + jnp.where(t == 3, 540, SHARD + 720 + 4 * t)
    tail = jnp.where(t == 0, 0, jnp.where(t == 1, 13, 10))
    level2 = step + jnp.where(t == 3, 855, SHARD + 720 + 192 + tail)
    spare = 3 * block + step - 45
    spare = jnp.where((t == 3) & (spare < 60) & (row < USED), 900 + spare, -1)
    live = jnp.where(row < L1_ROW, level0, jnp.where(row < L2_ROW, level1, level2))
    return jnp.where((step < 45) & (row < USED), live, spare)


def spread_source(start, t):
    row = lax.broadcasted_iota(jnp.int32, (240, 1), 0) + start
    at = 240 * t + row
    place = jnp.where(at < 720, at, at - 720)
    high = QUAD * (place & 3) + BLK * (place >> 2 & 3) + (place >> 4) + jnp.where(at < 720, 0, ROWS)
    first = (row >= 180).astype(jnp.int32) + (row >= 360).astype(jnp.int32) + (row >= 540).astype(jnp.int32)
    inside = row - 180 * first
    level1 = L1_ROW + BLK * (inside & 3) + (inside >> 2)
    rest = row - 720
    second = (rest >= 45).astype(jnp.int32) + (rest >= 90).astype(jnp.int32) + (rest >= 135).astype(jnp.int32)
    level2 = L2_ROW + rest - 45 * second
    spare = row - 900
    third = spare * 21846 >> 16
    low = jnp.where(row < 720, level1, level2)
    window = jnp.where(row < 720, first, second)
    low = jnp.where(window == 3, low, ROWS - L1_ROW + 240 * window + low)
    low = jnp.where(row < 900, low, BLK * third + 45 + spare - 3 * third)
    return jnp.where(t == 3, low, high)


def dot_nn(a, b):
    return jnp.dot(a, b, preferred_element_type=F32)


def dot_nt(a, b):
    return lax.dot_general(a, b, (((1,), (1,)), ((), ())), preferred_element_type=F32)


def dot_tn(a, b):
    return lax.dot_general(a, b, (((0,), (0,)), ((), ())), preferred_element_type=F32)


def one_hot(source, base, count):
    return (source - base == lax.broadcasted_iota(jnp.int32, (source.shape[0], count), 1)).astype(BF16)


def gathered_rows(start, t, own, recv, low):
    source = gather_source(start, t)
    total = dot_nn(one_hot(source, 0, SHARD), own[...])
    if start < L1_ROW:
        return total + dot_nn(one_hot(source, SHARD, 720), recv[...])
    return total + dot_nn(one_hot(source, SHARD + 720, 256), low[0][...] + low[1][...] + low[2][...])


def begin(sems, *pairs):
    copies = [pltpu.make_async_copy(src, dst, sems.at[i]) for i, (src, dst) in enumerate(pairs)]
    for copy in copies:
        copy.start()
    return copies


def finish(copies):
    for copy in copies:
        copy.wait()


def moments(values):
    center = values - jnp.mean(values, axis=-1, keepdims=True)
    spread = jnp.mean(center * center, axis=-1, keepdims=True)
    rstd = lax.rsqrt(spread + 1e-05)
    return center * rstd, rstd


def head_sum_matrix():
    row = lax.broadcasted_iota(jnp.int32, (8 * D, 128), 0)
    col = lax.broadcasted_iota(jnp.int32, (8 * D, 128), 1)
    return (row // DH == col % 64).astype(BF16)


def head_spread_matrix():
    row = lax.broadcasted_iota(jnp.int32, (128, 8 * D), 0)
    col = lax.broadcasted_iota(jnp.int32, (128, 8 * D), 1)
    return (row == col // DH).astype(BF16)


def slot_max(values):
    for step in (8, 16, 32):
        values = jnp.maximum(values, pltpu.roll(values, step, 1))
    return values


def slot_sum(values):
    for step in (8, 16, 32):
        values = values + pltpu.roll(values, step, 1)
    return values


def shift_down(block):
    row = lax.broadcasted_iota(jnp.int32, block.shape, 0)
    return jnp.where(row == 0, 0.0, pltpu.roll(block, 1, 0))


def shift_up(block):
    row = lax.broadcasted_iota(jnp.int32, block.shape, 0)
    return jnp.where(row == BLK - 1, 0.0, pltpu.roll(block, BLK - 1, 0))


def extend(ext, rows):
    kind = ext.dtype
    for c in range(4):
        ext[EXT_C[c] : EXT_C[c] + QUAD, :] = rows(QUAD * c, QUAD).astype(kind)
    ext[EXT_L1 : EXT_L1 + QUAD, :] = rows(L1_ROW, QUAD).astype(kind)
    last = rows(L2_ROW, BLK)
    ext[EXT_L2 : EXT_L2 + BLK, :] = last.astype(kind)
    ext[192:240, :] = shift_up(rows(0, BLK)).astype(kind)
    ext[624:672, :] = shift_down(rows(3 * QUAD + 144, BLK)).astype(kind)
    ext[864:912, :] = shift_down(rows(L1_ROW + 144, BLK)).astype(kind)
    ext[1104:1152, :] = shift_up(rows(L1_ROW, BLK)).astype(kind)
    ext[1152:1200, :] = shift_down(last).astype(kind)
    ext[1248:1296, :] = shift_up(last).astype(kind)


def present(count, level, child, live_steps):
    row = lax.broadcasted_iota(jnp.int32, (count, 128), 0)
    slot = lax.broadcasted_iota(jnp.int32, (count, 128), 1) % 64 // 8
    step = row
    for start in (BLK, 2 * BLK, 3 * BLK):
        if start < count:
            step = jnp.where(row >= start, row - start, step)
    here = step < live_steps
    if level == 0:
        here = here & (slot < 4)
    if level == 2:
        here = here & (slot != 3)
    if level > 0 or child == 0:
        here = here & ((slot != 1) | (row > 0))
    if level > 0 or child == 3:
        here = here & ((slot != 2) | (row < count - BLK) | (step + 1 < live_steps))
    return here


def groups(ext):
    def quad(at):
        return lambda: ext[at : at + QUAD, :]

    def block(at):
        return lambda: ext[at : at + BLK, :]

    def tiled(at):
        return lambda: jnp.concatenate([ext[at : at + BLK, :]] * 4, axis=0)

    out = []
    for c in range(4):
        out.append((QUAD * c, QUAD, 0, c, [quad(EXT_C[c]), quad(EXT_LEFT[c]), quad(EXT_RIGHT[c]), quad(EXT_L1)]))
    out.append(
        (L1_ROW, QUAD, 1, 0, [quad(EXT_L1), quad(864), quad(960), tiled(EXT_L2)] + [quad(EXT_C[c]) for c in range(4)])
    )
    children = [block(EXT_L1 + BLK * d) for d in range(4)]
    out.append((L2_ROW, BLK, 2, 0, [block(EXT_L2), block(1152), block(1248), None] + children))
    return out


def attention_forward(
    lengths, own, recv, low0, low1, low2, gain, shift, b_out, w_qkv, w_out, plane, other, *rest
):
    x_hbm, n_hbm, qkv_hbm, prob_out, ctx_out, mid_out, w_hbm = rest[:7]
    x_out, n_out, qkv_out, w_full, own_qkv, own_out, near, far, kx, vx, heads_in, heads_out, in_sems, out_sems = rest[7:]
    me, t = lax.axis_index("dp") & 7, lax.axis_index("tensor")
    live_steps = lengths[t] >> 4
    loading = begin(in_sems, (w_qkv, own_qkv), (w_out, own_out), (plane, near), (other, far))
    for start in range(0, ROWS, 256):
        run = slice(start, start + 256)
        rows = gathered_rows(start, t, own, recv, (low0, low1, low2))
        x_out[run, :] = rows.astype(BF16)
        n_out[run, :] = (moments(rows)[0] * gain[...] + shift[...]).astype(BF16)
    heads_in[...] = head_sum_matrix()
    heads_out[...] = head_spread_matrix()
    finish(loading)
    for i in range(3):
        w_full[i, :, 0:128] = own_qkv[i]
    w_full[3, 0:128, :] = own_out[...]
    for half, pieces in enumerate((near, far)):
        for k in range(4):
            parity = (me & 1) ^ half
            at = pl.multiple_of((2 * k + parity) * 64, 64)
            for s in range(1, 4):
                for i in range(3):
                    w_full[i, pl.ds(at, 64), 128 * s : 128 * s + 128] = pieces[k, s - 1, i]
                top = pl.multiple_of(128 * s + 64 * parity, 64)
                w_full[3, pl.ds(top, 64), 128 * k : 128 * k + 128] = pieces[k, s - 1, 3]
    for i in range(3):
        for start in range(0, ROWS, 512):
            run = slice(start, start + 512)
            qkv_out[i, run, :] = dot_nn(n_out[run, :], w_full[i]).astype(BF16)
    storing = begin(out_sems, (x_out, x_hbm), (n_out, n_hbm), (qkv_out, qkv_hbm), (w_full, w_hbm))
    extend(kx, lambda at, count: qkv_out[1, at : at + count, :].astype(F32))
    extend(vx, lambda at, count: qkv_out[2, at : at + count, :].astype(F32))
    ctx_out[USED:ROWS, :] = jnp.zeros((ROWS - USED, D), BF16)
    prob_out[USED:ROWS, :] = jnp.zeros((ROWS - USED, 128), F32)
    for (first, count, level, child, keys), (_, _, _, _, values) in zip(groups(kx), groups(vx)):
        query = qkv_out[0, first : first + count, :] * jnp.bfloat16(1.0 / math.sqrt(DH))
        slots = [s for s in range(len(keys)) if keys[s] is not None]
        score = jnp.zeros((count, 128), F32)
        for s in slots:
            score = score + dot_nn(query * keys[s](), heads_in[D * s : D * s + D, :])
        here = present(count, level, child, live_steps)
        score = jnp.where(here, score, -1000000000.0)
        weight = jnp.where(here, jnp.exp(score - slot_max(score)), 0.0)
        prob = weight / jnp.maximum(slot_sum(weight), 1.0)
        prob_out[first : first + count, :] = prob
        prob_low = prob.astype(BF16)
        context = jnp.zeros((count, D), F32)
        for s in slots:
            context = context + dot_nn(prob_low, heads_out[:, D * s : D * s + D]) * values[s]()
        ctx_out[first : first + count, :] = context.astype(BF16)
    for start in range(0, ROWS, 512):
        run = slice(start, start + 512)
        mid_out[run, :] = x_out[run, :].astype(F32) + dot_nn(ctx_out[run, :], w_full[3]) + b_out[...]
    finish(storing)


def feed_forward(
    own, recv, low0, low1, low2, mid, gain, shift, b_down, w_up, b_up, w_down, pieces, *rest
):
    y_quad, y_low, keep_hbm, send_hbm, gnorm, grad_hbm, grad_bias = rest[:7]
    up_w, down_w, up_t, down_t, bias, normed, grad, normed_t, grad_t = rest[7:16]
    act_s, gup_s, total, tmp, arrived, keep, send, in_sems, out_sems = rest[16:]
    me, t = lax.axis_index("dp") & 7, lax.axis_index("tensor")
    loading = begin(in_sems, (w_up, up_w.at[0]), (w_down, down_w.at[0]), (pieces, arrived))
    for start in range(0, ROWS, 256):
        run = slice(start, start + 256)
        low = (moments(mid[run, :])[0] * gain[...] + shift[...]).astype(BF16)
        normed[run, :] = low
        normed_t[:, run] = low.T
        cot = gathered_rows(start, t, own, recv, (low0, low1, low2)).astype(BF16)
        grad[run, :] = cot
        grad_t[:, run] = cot.T
    finish(loading)
    storing = begin(out_sems.at[8:9], (grad, grad_hbm))
    bias[0:1, :] = b_up[...].astype(F32)
    for piece in range(8):
        for s in range(1, 4):
            up_w[s, 64 * piece : 64 * piece + 64, :] = arrived[piece, s - 1, 0:64, :]
            down_w[s, 64 * piece : 64 * piece + 64, :] = arrived[piece, s - 1, 64:128, :]
    for s in range(1, 4):
        bias[s : s + 1, :] = arrived[0, s - 1, 128:129, :].astype(F32)

    for s in range(4):
        up_here, down_here = up_w[s], down_w[s]
        up_t[...] = up_here.T
        down_t[...] = down_here.T
        sums = jnp.zeros((1, D), F32)
        for start in range(0, ROWS, 512):
            run = slice(start, start + 512)
            pre = dot_nn(normed[run, :], up_here) + bias[pl.ds(s, 1), :]
            square = pre * pre
            root = math.sqrt(2.0 / math.pi)
            bent = jnp.tanh(pre * (root + (root * 0.044715) * square))
            half = 0.5 * pre
            act = (half + half * bent).astype(BF16)
            slope = (0.5 + 0.5 * bent) + half * (1.0 - bent * bent) * (root + (3.0 * root * 0.044715) * square)
            gup = (slope * dot_nn(grad[run, :], down_t[...])).astype(BF16)
            act_s[run, :] = act
            gup_s[run, :] = gup
            sums = sums + jnp.sum(gup.astype(F32), axis=0, keepdims=True)
            if s == 0:
                total[run, :] = dot_nn(act, down_here)
                gnorm[run, :] = dot_nn(gup, up_t[...])
            else:
                total[run, :] += dot_nn(act, down_here)
                gnorm[run, :] += dot_nn(gup, up_t[...])
        grad_bias[pl.ds(s, 1), :] = sums
        tmp[0] = dot_nn(normed_t[...], gup_s[...]).astype(BF16)
        tmp[1] = dot_nn(grad_t[...], act_s[...]).astype(BF16)
        slot = (t - s) & 3
        for half, target in enumerate((keep, send)):
            for k in range(4):
                at = pl.multiple_of((me ^ (2 * k + half)) * 64, 64)
                target[slot, k, 0:64, :] = tmp[0, pl.ds(at, 64), :]
                target[slot, k, 64:128, :] = tmp[1, pl.ds(at, 64), :]
        begin(out_sems.at[pl.ds(2 * s, 2)], (keep.at[slot], keep_hbm.at[slot]), (send.at[slot], send_hbm.at[slot]))
    for start in range(0, ROWS, 256):
        run = slice(start, start + 256)
        out = (mid[run, :] + (total[run, :] + b_down[...])).astype(BF16)
        if start < L1_ROW:
            y_quad[run, :] = out
        else:
            y_low[...] = out
    for s in range(4):
        pltpu.make_async_copy(keep.at[s], keep_hbm.at[s], out_sems.at[2 * s]).wait()
        pltpu.make_async_copy(send.at[s], send_hbm.at[s], out_sems.at[2 * s + 1]).wait()
    finish(storing)


def norm_backward(lengths, mid, gnorm, grad, gain, ctx, w_full, *rest):
    gmid, gcontext, gw_out, small = rest[:4]
    attn, w_here, ctx_here, sems = rest[4:]
    live_steps = lengths[lax.axis_index("tensor")] >> 4
    loading = begin(sems, (w_full.at[3], w_here), (ctx, ctx_here))
    finish(loading[:1])
    sums = [jnp.zeros((1, D), F32) for _ in range(4)]
    for start in range(0, ROWS, 256):
        run = slice(start, start + 256)
        hat, rstd = moments(mid[run, :])
        back = gnorm[run, :]
        scaled = back * gain[...]
        cot = grad[run, :].astype(F32)
        mean_one = jnp.mean(scaled, axis=-1, keepdims=True)
        mean_two = jnp.mean(scaled * hat, axis=-1, keepdims=True)
        result = cot + rstd * (scaled - mean_one - hat * mean_two)
        gmid[run, :] = result
        low = result.astype(BF16)
        attn[run, :] = low
        step = lax.broadcasted_iota(jnp.int32, (256, 1), 0) + start
        step = split_blocks(step)[1]
        gcontext[run, :] = jnp.where(step < live_steps, dot_nt(low, w_here[...]), 0.0).astype(BF16)
        terms = (cot, back * hat, back, low.astype(F32))
        sums = [running + jnp.sum(term, axis=0, keepdims=True) for running, term in zip(sums, terms)]
    finish(loading[1:])
    gw_out[...] = dot_tn(ctx_here[...], attn[...]).astype(BF16)
    small[...] = jnp.concatenate(sums + [jnp.zeros((4, D), F32)], axis=0)


def pair_sum(keep, far, *both):
    for k in range(4):
        for slot in range(4):
            both[k][slot] = (keep[slot, k].astype(F32) + far[slot, k].astype(F32)).astype(BF16)


REVERSE = (0, 2, 1)


def attention_backward(qkv, prob, gcontext, gain, small, small_up, gmid, x_in, n_in, gw_out, w_full, *rest):
    g_quad, g_low, keep, send = rest[:4]
    fx, cx, px, sx, heads_in, heads_out, packed, tmp = rest[4:12]
    bx, middle, x_here, n_here, gw_here, w_here, scores, sems = rest[12:]
    me, t = lax.axis_index("dp") & 7, lax.axis_index("tensor")
    loading = begin(sems, (gmid, middle), (x_in, x_here), (n_in, n_here), (gw_out, gw_here), (w_full, w_here))
    heads_in[...] = head_sum_matrix()
    heads_out[...] = head_spread_matrix()
    scale = 1.0 / math.sqrt(DH)
    extend(fx, lambda at, count: qkv[1, at : at + count, :].astype(F32))
    extend(bx, lambda at, count: qkv[2, at : at + count, :].astype(F32))
    packed[:, USED:ROWS, :] = jnp.zeros((3, ROWS - USED, D), BF16)
    for (first, count, level, child, keys), (_, _, _, _, values) in zip(groups(fx), groups(bx)):
        run = slice(first, first + count)
        slots = [s for s in range(len(keys)) if keys[s] is not None]
        cot = gcontext[run, :]
        gprob = jnp.zeros((count, 128), F32)
        for s in slots:
            gprob = gprob + dot_nn(cot * values[s](), heads_in[D * s : D * s + D, :])
        here = prob[run, :]
        gscore = (here * (gprob - slot_sum(here * gprob))).astype(BF16)
        scores[run, :] = gscore.astype(F32)
        gquery = jnp.zeros((count, D), F32)
        for s in slots:
            gquery = gquery + dot_nn(gscore, heads_out[:, D * s : D * s + D]) * keys[s]()
        packed[0, run, :] = (gquery * scale).astype(BF16)
    extend(fx, lambda at, count: qkv[0, at : at + count, :].astype(F32) * scale)
    extend(cx, lambda at, count: gcontext[at : at + count, :].astype(F32))
    extend(px, lambda at, count: prob[at : at + count, :])
    extend(sx, lambda at, count: scores[at : at + count, :])
    for quers, grads, probs, scors in zip(groups(fx), groups(cx), groups(px), groups(sx)):
        first, count, level, child, queries = quers
        gkey = jnp.zeros((count, D), F32)
        gvalue = jnp.zeros((count, D), F32)
        for s in range(len(queries)):
            if queries[s] is None:
                continue
            weight, score = probs[4][s](), scors[4][s]()
            if s < 3:
                back = REVERSE[s]
            elif s == 3:
                back = 4 + child
            else:
                back = 3
            if level == 1 and s == 3:
                wide_p = jnp.concatenate(
                    [dot_nn(weight[0:BLK, :], heads_out[:, D * (4 + d) : D * (5 + d)]) for d in range(4)], axis=0
                )
                wide_s = jnp.concatenate(
                    [dot_nn(score[0:BLK, :], heads_out[:, D * (4 + d) : D * (5 + d)]) for d in range(4)], axis=0
                )
            else:
                wide_p = dot_nn(weight, heads_out[:, D * back : D * back + D])
                wide_s = dot_nn(score, heads_out[:, D * back : D * back + D])
            gkey = gkey + wide_s * queries[s]()
            gvalue = gvalue + wide_p * grads[4][s]()
        packed[1, first : first + count, :] = gkey.astype(BF16)
        packed[2, first : first + count, :] = gvalue.astype(BF16)
    finish(loading)
    normed_t = n_here[...].T
    for i in range(3):
        tmp[i] = dot_nn(normed_t, packed[i]).astype(BF16)
    sums = [jnp.zeros((1, D), F32) for _ in range(2)]
    for start in range(0, ROWS, 256):
        run = slice(start, start + 256)
        back = dot_nt(packed[0, run, :], w_here[0])
        back = back + dot_nt(packed[1, run, :], w_here[1])
        back = back + dot_nt(packed[2, run, :], w_here[2])
        hat, rstd = moments(x_here[run, :].astype(F32))
        scaled = back * gain[...]
        mean_one = jnp.mean(scaled, axis=-1, keepdims=True)
        mean_two = jnp.mean(scaled * hat, axis=-1, keepdims=True)
        result = (middle[run, :] + rstd * (scaled - mean_one - hat * mean_two)).astype(BF16)
        if start < L1_ROW:
            g_quad[run, :] = result
        else:
            g_low[...] = result[0 : USED - L1_ROW, :]
        terms = (back * hat, back)
        sums = [running + jnp.sum(term, axis=0, keepdims=True) for running, term in zip(sums, terms)]
    sums = [small[i : i + 1, :] for i in range(4)] + sums
    for s in range(4):
        slot = ((t - s) & 3) ^ t
        vectors = sums + [small_up[s : s + 1, :]]
        rows = [vector[:, 128 * i : 128 * i + 128] for vector in vectors for i in range(4)]
        rows = jnp.concatenate(rows + [jnp.zeros((4, 128), F32)], axis=0).astype(BF16)
        for half, target in enumerate((keep, send)):
            for k in range(4):
                parity = (me & 1) ^ half
                at = pl.multiple_of((2 * k + parity) * 64, 64)
                for i in range(3):
                    target[k, slot, 64 * i : 64 * i + 64, :] = tmp[i, pl.ds(at, 64), 128 * s : 128 * s + 128]
                top = pl.multiple_of(128 * s + 64 * parity, 64)
                target[k, slot, 192:256, :] = gw_here[pl.ds(top, 64), 128 * k : 128 * k + 128]
                target[k, slot, 256:288, :] = rows


def spread_rows(quad, low, recv, *rest):
    t, (*lows, out) = lax.axis_index("tensor"), rest
    count = USED - L1_ROW
    if len(lows) == 3:
        others = [part[...] for part in lows]
    else:
        others = [jnp.where(t == 3, lows[0][w, 0:count, :], jnp.zeros((count, D), BF16)) for w in range(3)]
    moved = recv[...] + jnp.concatenate(others + [jnp.zeros((48, D), BF16)], axis=0)
    for start in range(0, SHARD, 240):
        source = spread_source(start, t)
        rows = dot_nn(one_hot(source, 0, L1_ROW), quad[...])
        rows = rows + dot_nn(one_hot(source, L1_ROW, count), low[0:count, :])
        rows = rows + dot_nn(one_hot(source, ROWS, L1_ROW), moved)
        out[start : start + 240, :] = rows.astype(out.dtype)


def unpack_weights(in_a, in_b, g_qkv, g_out, g_up, g_down, down_t):
    for p in range(8):
        g_up[64 * p : 64 * p + 64, :] = in_b[p, 0:64, :].astype(F32)
        down_t[64 * p : 64 * p + 64, :] = in_b[p, 64:128, :].astype(F32)
    g_down[...] = down_t[...].T
    for p in range(8):
        for i in range(3):
            g_qkv[i, 64 * p : 64 * p + 64, :] = in_a[p, 64 * i : 64 * i + 64, :].astype(F32)
        top, side = 64 * (p % 2), 128 * (p // 2)
        g_out[top : top + 64, side : side + 128] = in_a[p, 192:256, :].astype(F32)


def call(body, name, ins, outs, scratch=(), moved=1000, far_ins=(), far_outs=()):
    specs = [pl.BlockSpec(memory_space=pl.ANY if i in far_ins else pltpu.VMEM) for i in range(len(ins))]
    if ins[0].ndim == 1:
        specs[0] = pl.BlockSpec(memory_space=pltpu.SMEM)
    return pl.pallas_call(
        body,
        out_shape=tuple(outs),
        in_specs=specs,
        out_specs=tuple(pl.BlockSpec(memory_space=pl.ANY if i in far_outs else pltpu.VMEM) for i in range(len(outs))),
        scratch_shapes=list(scratch),
        compiler_params=pltpu.CompilerParams(vmem_limit_bytes=VMEM_BYTES),
        cost_estimate=pl.CostEstimate(flops=1000, bytes_accessed=moved, transcendentals=0),
        name=name,
    )(*ins)


def struct(shape, dtype):
    return jax.ShapeDtypeStruct(shape, dtype)


def shards(
    tokens,
    cotangent,
    lengths,
    neighbours,
    ln1_gain,
    ln1_shift,
    w_qkv,
    w_out,
    b_out,
    ln2_gain,
    ln2_shift,
    w_up,
    b_up,
    w_down,
    b_down,
    n_dp,
):
    sub = lax.axis_index("dp") & 7
    planes = [[8 * g + 2 * k + c for k in range(4)] for g in range(n_dp // 8) for c in range(2)]
    eights = [[8 * g + k for k in range(8)] for g in range(n_dp // 8)]

    def to_peer(value, e):
        return lax.ppermute(value, "dp", [(i, i ^ e) for i in range(n_dp)])

    def along(value, step):
        return lax.ppermute(value, "tensor", [(i, (i + step) % 4) for i in range(4)])

    def hop(value, pairs):
        return lax.ppermute(value, "tensor", pairs)

    def row(vec):
        return vec.reshape(1, -1)

    def after(values, *others):
        return lax.optimization_barrier((values, others))[0]

    def lower(terms):
        return sum(v.astype(F32) for v in terms).astype(BF16)

    act, wide = struct((ROWS, D), BF16), struct((ROWS, D), F32)
    quad_rows, low_rows = struct((L1_ROW, D), BF16), struct((USED - L1_ROW, D), BF16)
    extended, narrow = pltpu.VMEM((EXT, D), F32), pltpu.VMEM((EXT, 128), BF16)
    sum_heads, spread_heads = pltpu.VMEM((8 * D, 128), BF16), pltpu.VMEM((128, 8 * D), BF16)

    piece_a = jnp.concatenate(
        [
            lax.dynamic_slice(w_qkv, (0, 64 * sub, 0), (3, 64, 128)),
            lax.dynamic_slice(w_out, (64 * (sub % 2), 128 * (sub // 2)), (64, 128))[None],
        ],
        axis=0,
    )
    piece = jnp.concatenate(
        [
            lax.dynamic_slice(w_up, (64 * sub, 0), (64, D)),
            lax.dynamic_slice(w_down, (64 * sub, 0), (64, D)),
            row(b_up),
            jnp.zeros((15, D), BF16),
            piece_a.swapaxes(0, 1).reshape(64, D),
        ],
        axis=0,
    )
    arrived = [along(piece, s) for s in (1, 2, 3)]
    first_a = jnp.stack([v[144:].reshape(64, 4, 128).swapaxes(0, 1) for v in arrived])
    first_b = jnp.stack([v[:144] for v in arrived])
    plane_a = lax.all_gather(first_a, "dp", axis=0, axis_index_groups=planes)
    other_a = to_peer(plane_a, 1)
    pieces_b = lax.all_gather(first_b, "dp", axis=0, axis_index_groups=eights)

    def bring(rows, *others):
        cuts = [rows[SEND_LO:]]
        for w in range(3):
            cuts.append(jnp.concatenate([rows[at : at + size] for at, size in ((LOW_HEAD[w], 192), (LOW_TAIL[w], 64))]))
        cuts = after(cuts, *others)
        return [hop(cuts[0], [(0, 1), (1, 2), (2, 3)])] + [hop(cuts[1 + w], [(3, w)]) for w in range(3)]

    token_rows = bring(tokens, first_a)
    grad_rows = bring(cotangent, *token_rows)
    rows_low = pltpu.VMEM((ROWS, D), BF16)
    all_rows = pltpu.VMEM((3, ROWS, D), BF16)
    weights = pltpu.VMEM((4, D, D), BF16)
    piece_rows = pltpu.VMEM((4, 3, 4, 64, 128), BF16)
    low_extended = pltpu.VMEM((EXT, D), BF16)
    sems = pltpu.SemaphoreType.DMA
    x, n_one, qkv, prob, ctx, mid, w_full = call(
        attention_forward,
        "attention_forward",
        [lengths, tokens] + token_rows + [row(ln1_gain), row(ln1_shift), row(b_out), w_qkv, w_out, plane_a, other_a],
        [act, act, struct((3, ROWS, D), BF16), struct((ROWS, 128), F32), act, wide, struct((4, D, D), BF16)],
        [
            rows_low,
            rows_low,
            all_rows,
            weights,
            pltpu.VMEM((3, D, 128), BF16),
            pltpu.VMEM((128, D), BF16),
            piece_rows,
            piece_rows,
            low_extended,
            extended,
            sum_heads,
            spread_heads,
            sems((4,)),
            sems((4,)),
        ],
        far_ins=(9, 10, 11, 12),
        far_outs=(0, 1, 2, 6),
    )
    half_b = struct((4, 4, 128, D), BF16)
    square = pltpu.VMEM((D, D), BF16)
    turned = pltpu.VMEM((D, ROWS), BF16)
    y_quad, y_low, keep_b, send_b, gnorm, grad, small_up = call(
        feed_forward,
        "feed_forward",
        [cotangent]
        + grad_rows
        + [mid, row(ln2_gain), row(ln2_shift), row(b_down), w_up, row(b_up), w_down, pieces_b],
        [quad_rows, struct((256, D), BF16), half_b, half_b, wide, act, struct((4, D), F32)],
        [weights, weights, square, square, pltpu.VMEM((4, D), F32), rows_low, rows_low, turned, turned]
        + [rows_low, rows_low, pltpu.VMEM((ROWS, D), F32), pltpu.VMEM((2, D, D), BF16)]
        + [pltpu.VMEM((8, 3, 144, D), BF16), pltpu.VMEM((4, 4, 128, D), BF16), pltpu.VMEM((4, 4, 128, D), BF16)]
        + [sems((3,)), sems((9,))],
        far_ins=(9, 11, 12),
        far_outs=(2, 3, 5),
    )
    far_send = to_peer(send_b, 1)
    gmid, gcontext, gw_out, small = call(
        norm_backward,
        "norm_backward",
        [lengths, mid, gnorm, grad, row(ln2_gain), ctx, w_full],
        [wide, act, struct((D, D), BF16), struct((8, D), F32)],
        [rows_low, square, rows_low, sems((2,))],
        25000000,
        far_ins=(5, 6),
    )
    both_b = call(pair_sum, "pair_sum", [keep_b, after(far_send, small)], [struct((4, 128, D), BF16)] * 4)

    def across(value, bits):
        return lax.ppermute(value, "tensor", [(i, i ^ bits) for i in range(4)])

    def wider(plane):
        bit = 8
        while bit < n_dp:
            plane = [lower([v, to_peer(v, bit)]) for v in plane]
            bit *= 2
        return plane

    left = [(1, 0), (2, 1), (3, 2)]
    y_lows = [lax.all_gather(y_low, "tensor", axis=0)]
    y_recv = hop(y_quad, left)
    half_a = struct((4, 4, 288, 128), BF16)
    g_quad, g_low, keep_a, send_a = call(
        attention_backward,
        "attention_backward",
        [qkv, prob, gcontext, row(ln1_gain), small, small_up, gmid, x, n_one, gw_out, w_full],
        [quad_rows, low_rows, half_a, half_a],
        [extended, extended, narrow, narrow, sum_heads, spread_heads, all_rows, pltpu.VMEM((3, D, D), BF16)]
        + [low_extended, pltpu.VMEM((ROWS, D), F32), rows_low, rows_low, square, weights]
        + [pltpu.VMEM((ROWS, 128), F32), sems((5,))],
        60000000,
        far_ins=(6, 7, 8, 9, 10),
    )
    parts_b = after([both_b[0]] + [to_peer(both_b[k], 2 * k) for k in (1, 2, 3)], keep_a)
    far_a = to_peer(after(send_a, y_recv, *y_lows, *parts_b), 1)
    plane_b = wider([lower([v[s] for v in parts_b]) for s in range(4)])
    mine_b = lax.psum_scatter(jnp.concatenate(plane_b), "tensor", scatter_dimension=0, tiled=True)
    both_a = lower([keep_a, far_a])
    parts_a = lax.all_to_all(both_a, "dp", 0, 0, axis_index_groups=planes, tiled=True)
    g_lows = [hop(after(g_low, both_a), [(w, 3)]) for w in range(3)]
    g_recv = hop(after(g_quad, both_a), left)
    output = call(
        spread_rows, "spread_rows", [after(y_quad, both_a), y_low, y_recv] + y_lows, [struct((SHARD, D), BF16)]
    )[0]
    parts_a = after(parts_a, g_recv, output, *g_lows)
    plane_a = wider([lower([parts_a[i, s] for i in range(4)]) for s in range(4)])
    mine_b = after(mine_b, parts_a)
    flat_b = lax.all_gather(mine_b, "dp", axis=0, axis_index_groups=eights)
    mine_a = lower([plane_a[0]] + [across(plane_a[s], s) for s in (1, 2, 3)])
    grad_tokens = call(
        spread_rows, "spread_rows", [after(g_quad, parts_a), g_low, g_recv] + g_lows, [struct((SHARD, D), F32)]
    )[0]
    mine_a = after(mine_a, output, grad_tokens, mine_b)
    flat_a = lax.all_gather(mine_a, "dp", axis=0, axis_index_groups=eights)
    g_qkv, g_out, g_up, g_down = call(
        unpack_weights,
        "unpack_weights",
        [flat_a, flat_b],
        [struct((3, D, 128), F32), struct((128, D), F32), struct((D, D), F32), struct((D, D), F32)],
        [pltpu.VMEM((D, D), F32)],
    )
    sums = mine_a[256:284].astype(F32).reshape(7, D)
    return (
        output,
        grad_tokens,
        sums[4],
        sums[5],
        g_qkv,
        g_out,
        sums[3],
        sums[1],
        sums[2],
        g_up,
        sums[6],
        g_down,
        sums[0],
    )


def solution(mesh):
    n_dp = mesh.shape["dp"]
    placed = (
        P(("dp", "tensor"), None),
        P(("dp", "tensor"), None),
        P("dp"),
        P("dp", None),
        P(),
        P(),
        P(None, None, "tensor"),
        P("tensor", None),
        P(),
        P(),
        P(),
        P(None, "tensor"),
        P("tensor"),
        P("tensor", None),
        P(),
    )

    def run(*args):
        return shards(*args, n_dp)

    return jax.shard_map(
        run,
        mesh=mesh,
        in_specs=placed,
        out_specs=(
            P(("dp", "tensor"), None),
            P(("dp", "tensor"), None),
            P(),
            P(),
            P(None, None, "tensor"),
            P("tensor", None),
            P(),
            P(),
            P(),
            P(None, "tensor"),
            P("tensor"),
            P("tensor", None),
            P(),
        ),
        check_vma=False,
    )
```

```python
import math

import jax
import jax.numpy as jnp
from jax import lax
from jax.experimental import pallas as pl
from jax.experimental.pallas import tpu as pltpu
from jax.sharding import PartitionSpec as P

D = 512
DH = 64
MAXLEN = 720
NODES_GRP = 3840
SHARD = NODES_GRP // 4
F32 = jnp.float32
BF16 = jnp.bfloat16

BLK = 48
QUAD = 4 * BLK
L1_ROW = 4 * QUAD
L2_ROW = L1_ROW + QUAD
USED = L2_ROW + BLK
ROWS = 1024
EXT_C = (0, 240, 432, 672)
EXT_LEFT = (624, 0, 240, 432)
EXT_RIGHT = (240, 432, 672, 48)
EXT_L1 = 912
EXT_L2 = 1200
EXT = 1296
VMEM_BYTES = 60 * 1024 * 1024
SEND_LO = SHARD - MAXLEN
LOW_HEAD = (0, 176, 352)
LOW_TAIL = (720, 752, 800)


def split_blocks(row):
    block = row * 1366 >> 16
    return block, row - BLK * block


def gather_source(start, t):
    row = lax.broadcasted_iota(jnp.int32, (256, 1), 0) + start
    block, step = split_blocks(row)
    child, node = block >> 2, block & 3
    at = 720 - 240 * t + 16 * step + 4 * node + child
    level0 = jnp.where(at < 720, SHARD + at, at - 720)
    level1 = 4 * step + node + jnp.where(t == 3, 540, SHARD + 720 + 4 * t)
    tail = jnp.where(t == 0, 0, jnp.where(t == 1, 13, 10))
    level2 = step + jnp.where(t == 3, 855, SHARD + 720 + 192 + tail)
    spare = 3 * block + step - 45
    spare = jnp.where((t == 3) & (spare < 60) & (row < USED), 900 + spare, -1)
    live = jnp.where(row < L1_ROW, level0, jnp.where(row < L2_ROW, level1, level2))
    return jnp.where((step < 45) & (row < USED), live, spare)


def spread_source(start, t):
    row = lax.broadcasted_iota(jnp.int32, (240, 1), 0) + start
    at = 240 * t + row
    place = jnp.where(at < 720, at, at - 720)
    high = QUAD * (place & 3) + BLK * (place >> 2 & 3) + (place >> 4) + jnp.where(at < 720, 0, ROWS)
    first = (row >= 180).astype(jnp.int32) + (row >= 360).astype(jnp.int32) + (row >= 540).astype(jnp.int32)
    inside = row - 180 * first
    level1 = L1_ROW + BLK * (inside & 3) + (inside >> 2)
    rest = row - 720
    second = (rest >= 45).astype(jnp.int32) + (rest >= 90).astype(jnp.int32) + (rest >= 135).astype(jnp.int32)
    level2 = L2_ROW + rest - 45 * second
    spare = row - 900
    third = spare * 21846 >> 16
    low = jnp.where(row < 720, level1, level2)
    window = jnp.where(row < 720, first, second)
    low = jnp.where(window == 3, low, ROWS - L1_ROW + 240 * window + low)
    low = jnp.where(row < 900, low, BLK * third + 45 + spare - 3 * third)
    return jnp.where(t == 3, low, high)


def dot_nn(a, b):
    return jnp.dot(a, b, preferred_element_type=F32)


def dot_nt(a, b):
    return lax.dot_general(a, b, (((1,), (1,)), ((), ())), preferred_element_type=F32)


def dot_tn(a, b):
    return lax.dot_general(a, b, (((0,), (0,)), ((), ())), preferred_element_type=F32)


def one_hot(source, base, count):
    return (source - base == lax.broadcasted_iota(jnp.int32, (source.shape[0], count), 1)).astype(BF16)


def gathered_rows(start, t, own, recv, low):
    source = gather_source(start, t)
    total = dot_nn(one_hot(source, 0, SHARD), own[...])
    if start < L1_ROW:
        return total + dot_nn(one_hot(source, SHARD, 720), recv[...])
    return total + dot_nn(one_hot(source, SHARD + 720, 256), low[0][...] + low[1][...] + low[2][...])


def begin(sems, *pairs):
    copies = [pltpu.make_async_copy(src, dst, sems.at[i]) for i, (src, dst) in enumerate(pairs)]
    for copy in copies:
        copy.start()
    return copies


def finish(copies):
    for copy in copies:
        copy.wait()


def moments(values):
    center = values - jnp.mean(values, axis=-1, keepdims=True)
    spread = jnp.mean(center * center, axis=-1, keepdims=True)
    rstd = lax.rsqrt(spread + 1e-05)
    return center * rstd, rstd


def head_sum_matrix():
    row = lax.broadcasted_iota(jnp.int32, (8 * D, 128), 0)
    col = lax.broadcasted_iota(jnp.int32, (8 * D, 128), 1)
    return (row // DH == col % 64).astype(BF16)


def head_spread_matrix():
    row = lax.broadcasted_iota(jnp.int32, (128, 8 * D), 0)
    col = lax.broadcasted_iota(jnp.int32, (128, 8 * D), 1)
    return (row == col // DH).astype(BF16)


def slot_max(values):
    for step in (8, 16, 32):
        values = jnp.maximum(values, pltpu.roll(values, step, 1))
    return values


def slot_sum(values):
    for step in (8, 16, 32):
        values = values + pltpu.roll(values, step, 1)
    return values


def shift_down(block):
    row = lax.broadcasted_iota(jnp.int32, block.shape, 0)
    return jnp.where(row == 0, 0.0, pltpu.roll(block, 1, 0))


def shift_up(block):
    row = lax.broadcasted_iota(jnp.int32, block.shape, 0)
    return jnp.where(row == BLK - 1, 0.0, pltpu.roll(block, BLK - 1, 0))


def extend(ext, rows):
    kind = ext.dtype
    for c in range(4):
        ext[EXT_C[c] : EXT_C[c] + QUAD, :] = rows(QUAD * c, QUAD).astype(kind)
    ext[EXT_L1 : EXT_L1 + QUAD, :] = rows(L1_ROW, QUAD).astype(kind)
    last = rows(L2_ROW, BLK)
    ext[EXT_L2 : EXT_L2 + BLK, :] = last.astype(kind)
    ext[192:240, :] = shift_up(rows(0, BLK)).astype(kind)
    ext[624:672, :] = shift_down(rows(3 * QUAD + 144, BLK)).astype(kind)
    ext[864:912, :] = shift_down(rows(L1_ROW + 144, BLK)).astype(kind)
    ext[1104:1152, :] = shift_up(rows(L1_ROW, BLK)).astype(kind)
    ext[1152:1200, :] = shift_down(last).astype(kind)
    ext[1248:1296, :] = shift_up(last).astype(kind)


def present(count, level, child, live_steps):
    row = lax.broadcasted_iota(jnp.int32, (count, 128), 0)
    slot = lax.broadcasted_iota(jnp.int32, (count, 128), 1) % 64 // 8
    step = row
    for start in (BLK, 2 * BLK, 3 * BLK):
        if start < count:
            step = jnp.where(row >= start, row - start, step)
    here = step < live_steps
    if level == 0:
        here = here & (slot < 4)
    if level == 2:
        here = here & (slot != 3)
    if level > 0 or child == 0:
        here = here & ((slot != 1) | (row > 0))
    if level > 0 or child == 3:
        here = here & ((slot != 2) | (row < count - BLK) | (step + 1 < live_steps))
    return here


def groups(ext):
    def quad(at):
        return lambda: ext[at : at + QUAD, :]

    def block(at):
        return lambda: ext[at : at + BLK, :]

    def tiled(at):
        return lambda: jnp.concatenate([ext[at : at + BLK, :]] * 4, axis=0)

    out = []
    for c in range(4):
        out.append((QUAD * c, QUAD, 0, c, [quad(EXT_C[c]), quad(EXT_LEFT[c]), quad(EXT_RIGHT[c]), quad(EXT_L1)]))
    out.append(
        (L1_ROW, QUAD, 1, 0, [quad(EXT_L1), quad(864), quad(960), tiled(EXT_L2)] + [quad(EXT_C[c]) for c in range(4)])
    )
    children = [block(EXT_L1 + BLK * d) for d in range(4)]
    out.append((L2_ROW, BLK, 2, 0, [block(EXT_L2), block(1152), block(1248), None] + children))
    return out


def attention_forward(
    lengths, own, recv, low0, low1, low2, gain, shift, b_out, w_qkv, w_out, plane, other, *rest
):
    x_hbm, n_hbm, qkv_hbm, prob_out, ctx_out, mid_out, w_hbm = rest[:7]
    x_out, n_out, qkv_out, w_full, own_qkv, own_out, near, far, kx, vx, heads_in, heads_out, in_sems, out_sems = rest[7:]
    me, t = lax.axis_index("dp") & 7, lax.axis_index("tensor")
    live_steps = lengths[t] >> 4
    loading = begin(in_sems, (w_qkv, own_qkv), (w_out, own_out), (plane, near), (other, far))
    for start in range(0, ROWS, 256):
        run = slice(start, start + 256)
        rows = gathered_rows(start, t, own, recv, (low0, low1, low2))
        x_out[run, :] = rows.astype(BF16)
        n_out[run, :] = (moments(rows)[0] * gain[...] + shift[...]).astype(BF16)
    heads_in[...] = head_sum_matrix()
    heads_out[...] = head_spread_matrix()
    finish(loading)
    for i in range(3):
        w_full[i, :, 0:128] = own_qkv[i]
    w_full[3, 0:128, :] = own_out[...]
    for half, pieces in enumerate((near, far)):
        for k in range(4):
            parity = (me & 1) ^ half
            at = pl.multiple_of((2 * k + parity) * 64, 64)
            for s in range(1, 4):
                for i in range(3):
                    w_full[i, pl.ds(at, 64), 128 * s : 128 * s + 128] = pieces[k, s - 1, i]
                top = pl.multiple_of(128 * s + 64 * parity, 64)
                w_full[3, pl.ds(top, 64), 128 * k : 128 * k + 128] = pieces[k, s - 1, 3]
    for i in range(3):
        for start in range(0, ROWS, 512):
            run = slice(start, start + 512)
            qkv_out[i, run, :] = dot_nn(n_out[run, :], w_full[i]).astype(BF16)
    storing = begin(out_sems, (x_out, x_hbm), (n_out, n_hbm), (qkv_out, qkv_hbm), (w_full, w_hbm))
    extend(kx, lambda at, count: qkv_out[1, at : at + count, :].astype(F32))
    extend(vx, lambda at, count: qkv_out[2, at : at + count, :].astype(F32))
    ctx_out[USED:ROWS, :] = jnp.zeros((ROWS - USED, D), BF16)
    prob_out[USED:ROWS, :] = jnp.zeros((ROWS - USED, 128), F32)
    for (first, count, level, child, keys), (_, _, _, _, values) in zip(groups(kx), groups(vx)):
        query = qkv_out[0, first : first + count, :] * jnp.bfloat16(1.0 / math.sqrt(DH))
        slots = [s for s in range(len(keys)) if keys[s] is not None]
        score = jnp.zeros((count, 128), F32)
        for s in slots:
            score = score + dot_nn(query * keys[s](), heads_in[D * s : D * s + D, :])
        here = present(count, level, child, live_steps)
        score = jnp.where(here, score, -1000000000.0)
        weight = jnp.where(here, jnp.exp(score - slot_max(score)), 0.0)
        prob = weight / jnp.maximum(slot_sum(weight), 1.0)
        prob_out[first : first + count, :] = prob
        prob_low = prob.astype(BF16)
        context = jnp.zeros((count, D), F32)
        for s in slots:
            context = context + dot_nn(prob_low, heads_out[:, D * s : D * s + D]) * values[s]()
        ctx_out[first : first + count, :] = context.astype(BF16)
    for start in range(0, ROWS, 512):
        run = slice(start, start + 512)
        mid_out[run, :] = x_out[run, :].astype(F32) + dot_nn(ctx_out[run, :], w_full[3]) + b_out[...]
    finish(storing)


def feed_forward(
    own, recv, low0, low1, low2, mid, gain, shift, b_down, w_up, b_up, w_down, pieces, *rest
):
    y_quad, y_low, keep_hbm, send_hbm, gnorm_hbm, grad_hbm, grad_bias = rest[:7]
    up_w, down_w, up_t, down_t, bias, normed, grad, normed_t, grad_t = rest[7:16]
    act_s, gup_s, total, gnorm, tmp, arrived, keep, send, in_sems, out_sems = rest[16:]
    me, t = lax.axis_index("dp") & 7, lax.axis_index("tensor")
    loading = begin(in_sems, (w_up, up_w.at[0]), (w_down, down_w.at[0]), (pieces, arrived))
    for start in range(0, ROWS, 256):
        run = slice(start, start + 256)
        low = (moments(mid[run, :])[0] * gain[...] + shift[...]).astype(BF16)
        normed[run, :] = low
        normed_t[:, run] = low.T
        cot = gathered_rows(start, t, own, recv, (low0, low1, low2)).astype(BF16)
        grad[run, :] = cot
        grad_t[:, run] = cot.T
    finish(loading)
    storing = begin(out_sems.at[8:9], (grad, grad_hbm))
    bias[0:1, :] = b_up[...].astype(F32)
    for piece in range(8):
        for s in range(1, 4):
            up_w[s, 64 * piece : 64 * piece + 64, :] = arrived[piece, s - 1, 0:64, :]
            down_w[s, 64 * piece : 64 * piece + 64, :] = arrived[piece, s - 1, 64:128, :]
    for s in range(1, 4):
        bias[s : s + 1, :] = arrived[0, s - 1, 128:129, :].astype(F32)

    for s in range(4):
        up_here, down_here = up_w[s], down_w[s]
        up_t[...] = up_here.T
        down_t[...] = down_here.T
        sums = jnp.zeros((1, D), F32)
        for start in range(0, ROWS, 512):
            run = slice(start, start + 512)
            pre = dot_nn(normed[run, :], up_here) + bias[pl.ds(s, 1), :]
            square = pre * pre
            root = math.sqrt(2.0 / math.pi)
            bent = jnp.tanh(pre * (root + (root * 0.044715) * square))
            half = 0.5 * pre
            act = (half + half * bent).astype(BF16)
            slope = (0.5 + 0.5 * bent) + half * (1.0 - bent * bent) * (root + (3.0 * root * 0.044715) * square)
            gup = (slope * dot_nn(grad[run, :], down_t[...])).astype(BF16)
            act_s[run, :] = act
            gup_s[run, :] = gup
            sums = sums + jnp.sum(gup.astype(F32), axis=0, keepdims=True)
            if s == 0:
                total[run, :] = dot_nn(act, down_here)
                gnorm[run, :] = dot_nn(gup, up_t[...])
            else:
                total[run, :] += dot_nn(act, down_here)
                gnorm[run, :] += dot_nn(gup, up_t[...])
        grad_bias[pl.ds(s, 1), :] = sums
        tmp[0] = dot_nn(normed_t[...], gup_s[...]).astype(BF16)
        tmp[1] = dot_nn(grad_t[...], act_s[...]).astype(BF16)
        slot = (t - s) & 3
        for half, target in enumerate((keep, send)):
            for k in range(4):
                at = pl.multiple_of((me ^ (2 * k + half)) * 64, 64)
                target[slot, k, 0:64, :] = tmp[0, pl.ds(at, 64), :]
                target[slot, k, 64:128, :] = tmp[1, pl.ds(at, 64), :]
        begin(out_sems.at[pl.ds(2 * s, 2)], (keep.at[slot], keep_hbm.at[slot]), (send.at[slot], send_hbm.at[slot]))
    storing += begin(out_sems.at[9:10], (gnorm, gnorm_hbm))
    for start in range(0, ROWS, 256):
        run = slice(start, start + 256)
        out = (mid[run, :] + (total[run, :] + b_down[...])).astype(BF16)
        if start < L1_ROW:
            y_quad[run, :] = out
        else:
            y_low[...] = out
    for s in range(4):
        pltpu.make_async_copy(keep.at[s], keep_hbm.at[s], out_sems.at[2 * s]).wait()
        pltpu.make_async_copy(send.at[s], send_hbm.at[s], out_sems.at[2 * s + 1]).wait()
    finish(storing)


def norm_backward(lengths, mid, gnorm, grad, gain, ctx, w_full, *rest):
    gmid, gcontext, gw_out, small = rest[:4]
    attn, w_here, ctx_here, sems = rest[4:]
    live_steps = lengths[lax.axis_index("tensor")] >> 4
    loading = begin(sems, (w_full.at[3], w_here), (ctx, ctx_here))
    finish(loading[:1])
    sums = [jnp.zeros((1, D), F32) for _ in range(4)]
    for start in range(0, ROWS, 256):
        run = slice(start, start + 256)
        hat, rstd = moments(mid[run, :])
        back = gnorm[run, :]
        scaled = back * gain[...]
        cot = grad[run, :].astype(F32)
        mean_one = jnp.mean(scaled, axis=-1, keepdims=True)
        mean_two = jnp.mean(scaled * hat, axis=-1, keepdims=True)
        result = cot + rstd * (scaled - mean_one - hat * mean_two)
        gmid[run, :] = result
        low = result.astype(BF16)
        attn[run, :] = low
        step = lax.broadcasted_iota(jnp.int32, (256, 1), 0) + start
        step = split_blocks(step)[1]
        gcontext[run, :] = jnp.where(step < live_steps, dot_nt(low, w_here[...]), 0.0).astype(BF16)
        terms = (cot, back * hat, back, low.astype(F32))
        sums = [running + jnp.sum(term, axis=0, keepdims=True) for running, term in zip(sums, terms)]
    finish(loading[1:])
    gw_out[...] = dot_tn(ctx_here[...], attn[...]).astype(BF16)
    small[...] = jnp.concatenate(sums + [jnp.zeros((4, D), F32)], axis=0)


def pair_sum(keep, far, *both):
    for k in range(4):
        for slot in range(4):
            both[k][slot] = (keep[slot, k].astype(F32) + far[slot, k].astype(F32)).astype(BF16)


REVERSE = (0, 2, 1)


def attention_backward(qkv, prob, gcontext, gain, small, small_up, gmid, x_in, n_in, gw_out, w_full, *rest):
    g_quad, g_low, keep, send = rest[:4]
    fx, cx, px, sx, heads_in, heads_out, packed, tmp = rest[4:12]
    bx, middle, x_here, n_here, gw_here, w_here, scores, sems = rest[12:]
    me, t = lax.axis_index("dp") & 7, lax.axis_index("tensor")
    loading = begin(sems, (gmid, middle), (x_in, x_here), (n_in, n_here), (gw_out, gw_here), (w_full, w_here))
    heads_in[...] = head_sum_matrix()
    heads_out[...] = head_spread_matrix()
    scale = 1.0 / math.sqrt(DH)
    extend(fx, lambda at, count: qkv[1, at : at + count, :].astype(F32))
    extend(bx, lambda at, count: qkv[2, at : at + count, :].astype(F32))
    packed[:, USED:ROWS, :] = jnp.zeros((3, ROWS - USED, D), BF16)
    for (first, count, level, child, keys), (_, _, _, _, values) in zip(groups(fx), groups(bx)):
        run = slice(first, first + count)
        slots = [s for s in range(len(keys)) if keys[s] is not None]
        cot = gcontext[run, :]
        gprob = jnp.zeros((count, 128), F32)
        for s in slots:
            gprob = gprob + dot_nn(cot * values[s](), heads_in[D * s : D * s + D, :])
        here = prob[run, :]
        gscore = (here * (gprob - slot_sum(here * gprob))).astype(BF16)
        scores[run, :] = gscore.astype(F32)
        gquery = jnp.zeros((count, D), F32)
        for s in slots:
            gquery = gquery + dot_nn(gscore, heads_out[:, D * s : D * s + D]) * keys[s]()
        packed[0, run, :] = (gquery * scale).astype(BF16)
    extend(fx, lambda at, count: qkv[0, at : at + count, :].astype(F32) * scale)
    extend(cx, lambda at, count: gcontext[at : at + count, :].astype(F32))
    extend(px, lambda at, count: prob[at : at + count, :])
    extend(sx, lambda at, count: scores[at : at + count, :])
    for quers, grads, probs, scors in zip(groups(fx), groups(cx), groups(px), groups(sx)):
        first, count, level, child, queries = quers
        gkey = jnp.zeros((count, D), F32)
        gvalue = jnp.zeros((count, D), F32)
        for s in range(len(queries)):
            if queries[s] is None:
                continue
            weight, score = probs[4][s](), scors[4][s]()
            if s < 3:
                back = REVERSE[s]
            elif s == 3:
                back = 4 + child
            else:
                back = 3
            if level == 1 and s == 3:
                wide_p = jnp.concatenate(
                    [dot_nn(weight[0:BLK, :], heads_out[:, D * (4 + d) : D * (5 + d)]) for d in range(4)], axis=0
                )
                wide_s = jnp.concatenate(
                    [dot_nn(score[0:BLK, :], heads_out[:, D * (4 + d) : D * (5 + d)]) for d in range(4)], axis=0
                )
            else:
                wide_p = dot_nn(weight, heads_out[:, D * back : D * back + D])
                wide_s = dot_nn(score, heads_out[:, D * back : D * back + D])
            gkey = gkey + wide_s * queries[s]()
            gvalue = gvalue + wide_p * grads[4][s]()
        packed[1, first : first + count, :] = gkey.astype(BF16)
        packed[2, first : first + count, :] = gvalue.astype(BF16)
    finish(loading)
    normed_t = n_here[...].T
    for i in range(3):
        tmp[i] = dot_nn(normed_t, packed[i]).astype(BF16)
    sums = [jnp.zeros((1, D), F32) for _ in range(2)]
    for start in range(0, ROWS, 256):
        run = slice(start, start + 256)
        back = dot_nt(packed[0, run, :], w_here[0])
        back = back + dot_nt(packed[1, run, :], w_here[1])
        back = back + dot_nt(packed[2, run, :], w_here[2])
        hat, rstd = moments(x_here[run, :].astype(F32))
        scaled = back * gain[...]
        mean_one = jnp.mean(scaled, axis=-1, keepdims=True)
        mean_two = jnp.mean(scaled * hat, axis=-1, keepdims=True)
        result = (middle[run, :] + rstd * (scaled - mean_one - hat * mean_two)).astype(BF16)
        if start < L1_ROW:
            g_quad[run, :] = result
        else:
            g_low[...] = result[0 : USED - L1_ROW, :]
        terms = (back * hat, back)
        sums = [running + jnp.sum(term, axis=0, keepdims=True) for running, term in zip(sums, terms)]
    sums = [small[i : i + 1, :] for i in range(4)] + sums
    for s in range(4):
        slot = ((t - s) & 3) ^ t
        vectors = sums + [small_up[s : s + 1, :]]
        rows = [vector[:, 128 * i : 128 * i + 128] for vector in vectors for i in range(4)]
        rows = jnp.concatenate(rows + [jnp.zeros((4, 128), F32)], axis=0).astype(BF16)
        for half, target in enumerate((keep, send)):
            for k in range(4):
                parity = (me & 1) ^ half
                at = pl.multiple_of((2 * k + parity) * 64, 64)
                for i in range(3):
                    target[k, slot, 64 * i : 64 * i + 64, :] = tmp[i, pl.ds(at, 64), 128 * s : 128 * s + 128]
                top = pl.multiple_of(128 * s + 64 * parity, 64)
                target[k, slot, 192:256, :] = gw_here[pl.ds(top, 64), 128 * k : 128 * k + 128]
                target[k, slot, 256:288, :] = rows


def spread_rows(quad, low, recv, *rest):
    t, (*lows, out) = lax.axis_index("tensor"), rest
    count = USED - L1_ROW
    if len(lows) == 3:
        others = [part[...] for part in lows]
    else:
        others = [jnp.where(t == 3, lows[0][w, 0:count, :], jnp.zeros((count, D), BF16)) for w in range(3)]
    moved = recv[...] + jnp.concatenate(others + [jnp.zeros((48, D), BF16)], axis=0)
    for start in range(0, SHARD, 240):
        source = spread_source(start, t)
        rows = dot_nn(one_hot(source, 0, L1_ROW), quad[...])
        rows = rows + dot_nn(one_hot(source, L1_ROW, count), low[0:count, :])
        rows = rows + dot_nn(one_hot(source, ROWS, L1_ROW), moved)
        out[start : start + 240, :] = rows.astype(out.dtype)


def unpack_weights(in_a, in_b, *rest):
    outs, (g_qkv, g_out, g_up, g_down, down_t, sems) = rest[:4], rest[4:]
    for p in range(8):
        g_up[64 * p : 64 * p + 64, :] = in_b[p, 0:64, :].astype(F32)
        down_t[64 * p : 64 * p + 64, :] = in_b[p, 64:128, :].astype(F32)
    storing = begin(sems.at[0:1], (g_up, outs[2]))
    g_down[...] = down_t[...].T
    storing += begin(sems.at[1:2], (g_down, outs[3]))
    for p in range(8):
        for i in range(3):
            g_qkv[i, 64 * p : 64 * p + 64, :] = in_a[p, 64 * i : 64 * i + 64, :].astype(F32)
        top, side = 64 * (p % 2), 128 * (p // 2)
        g_out[top : top + 64, side : side + 128] = in_a[p, 192:256, :].astype(F32)
    storing += begin(sems.at[2:4], (g_qkv, outs[0]), (g_out, outs[1]))
    finish(storing)


def call(body, name, ins, outs, scratch=(), moved=1000, far_ins=(), far_outs=()):
    specs = [pl.BlockSpec(memory_space=pl.ANY if i in far_ins else pltpu.VMEM) for i in range(len(ins))]
    if ins[0].ndim == 1:
        specs[0] = pl.BlockSpec(memory_space=pltpu.SMEM)
    return pl.pallas_call(
        body,
        out_shape=tuple(outs),
        in_specs=specs,
        out_specs=tuple(pl.BlockSpec(memory_space=pl.ANY if i in far_outs else pltpu.VMEM) for i in range(len(outs))),
        scratch_shapes=list(scratch),
        compiler_params=pltpu.CompilerParams(vmem_limit_bytes=VMEM_BYTES),
        cost_estimate=pl.CostEstimate(flops=1000, bytes_accessed=moved, transcendentals=0),
        name=name,
    )(*ins)


def struct(shape, dtype):
    return jax.ShapeDtypeStruct(shape, dtype)


def shards(
    tokens,
    cotangent,
    lengths,
    neighbours,
    ln1_gain,
    ln1_shift,
    w_qkv,
    w_out,
    b_out,
    ln2_gain,
    ln2_shift,
    w_up,
    b_up,
    w_down,
    b_down,
    n_dp,
):
    sub = lax.axis_index("dp") & 7
    planes = [[8 * g + 2 * k + c for k in range(4)] for g in range(n_dp // 8) for c in range(2)]
    eights = [[8 * g + k for k in range(8)] for g in range(n_dp // 8)]

    def to_peer(value, e):
        return lax.ppermute(value, "dp", [(i, i ^ e) for i in range(n_dp)])

    def along(value, step):
        return lax.ppermute(value, "tensor", [(i, (i + step) % 4) for i in range(4)])

    def hop(value, pairs):
        return lax.ppermute(value, "tensor", pairs)

    def row(vec):
        return vec.reshape(1, -1)

    def after(values, *others):
        return lax.optimization_barrier((values, others))[0]

    def lower(terms):
        return sum(v.astype(F32) for v in terms).astype(BF16)

    act, wide = struct((ROWS, D), BF16), struct((ROWS, D), F32)
    quad_rows, low_rows = struct((L1_ROW, D), BF16), struct((USED - L1_ROW, D), BF16)
    extended, narrow = pltpu.VMEM((EXT, D), F32), pltpu.VMEM((EXT, 128), BF16)
    sum_heads, spread_heads = pltpu.VMEM((8 * D, 128), BF16), pltpu.VMEM((128, 8 * D), BF16)

    piece_a = jnp.concatenate(
        [
            lax.dynamic_slice(w_qkv, (0, 64 * sub, 0), (3, 64, 128)),
            lax.dynamic_slice(w_out, (64 * (sub % 2), 128 * (sub // 2)), (64, 128))[None],
        ],
        axis=0,
    )
    piece = jnp.concatenate(
        [
            lax.dynamic_slice(w_up, (64 * sub, 0), (64, D)),
            lax.dynamic_slice(w_down, (64 * sub, 0), (64, D)),
            row(b_up),
            jnp.zeros((15, D), BF16),
            piece_a.swapaxes(0, 1).reshape(64, D),
        ],
        axis=0,
    )
    arrived = [along(piece, s) for s in (1, 2, 3)]
    first_a = jnp.stack([v[144:].reshape(64, 4, 128).swapaxes(0, 1) for v in arrived])
    first_b = jnp.stack([v[:144] for v in arrived])
    plane_a = lax.all_gather(first_a, "dp", axis=0, axis_index_groups=planes)
    other_a = to_peer(plane_a, 1)
    pieces_b = lax.all_gather(first_b, "dp", axis=0, axis_index_groups=eights)

    def bring(rows, *others):
        cuts = [rows[SEND_LO:]]
        for w in range(3):
            cuts.append(jnp.concatenate([rows[at : at + size] for at, size in ((LOW_HEAD[w], 192), (LOW_TAIL[w], 64))]))
        cuts = after(cuts, *others)
        return [hop(cuts[0], [(0, 1), (1, 2), (2, 3)])] + [hop(cuts[1 + w], [(3, w)]) for w in range(3)]

    token_rows = bring(tokens, first_a)
    grad_rows = bring(cotangent, *token_rows)
    rows_low = pltpu.VMEM((ROWS, D), BF16)
    all_rows = pltpu.VMEM((3, ROWS, D), BF16)
    weights = pltpu.VMEM((4, D, D), BF16)
    piece_rows = pltpu.VMEM((4, 3, 4, 64, 128), BF16)
    low_extended = pltpu.VMEM((EXT, D), BF16)
    sems = pltpu.SemaphoreType.DMA
    x, n_one, qkv, prob, ctx, mid, w_full = call(
        attention_forward,
        "attention_forward",
        [lengths, tokens] + token_rows + [row(ln1_gain), row(ln1_shift), row(b_out), w_qkv, w_out, plane_a, other_a],
        [act, act, struct((3, ROWS, D), BF16), struct((ROWS, 128), F32), act, wide, struct((4, D, D), BF16)],
        [
            rows_low,
            rows_low,
            all_rows,
            weights,
            pltpu.VMEM((3, D, 128), BF16),
            pltpu.VMEM((128, D), BF16),
            piece_rows,
            piece_rows,
            low_extended,
            extended,
            sum_heads,
            spread_heads,
            sems((4,)),
            sems((4,)),
        ],
        far_ins=(9, 10, 11, 12),
        far_outs=(0, 1, 2, 6),
    )
    half_b = struct((4, 4, 128, D), BF16)
    square = pltpu.VMEM((D, D), BF16)
    turned = pltpu.VMEM((D, ROWS), BF16)
    y_quad, y_low, keep_b, send_b, gnorm, grad, small_up = call(
        feed_forward,
        "feed_forward",
        [cotangent]
        + grad_rows
        + [mid, row(ln2_gain), row(ln2_shift), row(b_down), w_up, row(b_up), w_down, pieces_b],
        [quad_rows, struct((256, D), BF16), half_b, half_b, wide, act, struct((4, D), F32)],
        [weights, weights, square, square, pltpu.VMEM((4, D), F32), rows_low, rows_low, turned, turned]
        + [rows_low, rows_low, pltpu.VMEM((ROWS, D), F32), pltpu.VMEM((ROWS, D), F32), pltpu.VMEM((2, D, D), BF16)]
        + [pltpu.VMEM((8, 3, 144, D), BF16), pltpu.VMEM((4, 4, 128, D), BF16), pltpu.VMEM((4, 4, 128, D), BF16)]
        + [sems((3,)), sems((10,))],
        far_ins=(9, 11, 12),
        far_outs=(2, 3, 4, 5),
    )
    far_send = to_peer(send_b, 1)
    gmid, gcontext, gw_out, small = call(
        norm_backward,
        "norm_backward",
        [lengths, mid, gnorm, grad, row(ln2_gain), ctx, w_full],
        [wide, act, struct((D, D), BF16), struct((8, D), F32)],
        [rows_low, square, rows_low, sems((2,))],
        25000000,
        far_ins=(5, 6),
    )
    both_b = call(pair_sum, "pair_sum", [keep_b, after(far_send, small)], [struct((4, 128, D), BF16)] * 4)

    def across(value, bits):
        return lax.ppermute(value, "tensor", [(i, i ^ bits) for i in range(4)])

    def wider(plane):
        bit = 8
        while bit < n_dp:
            plane = [lower([v, to_peer(v, bit)]) for v in plane]
            bit *= 2
        return plane

    left = [(1, 0), (2, 1), (3, 2)]
    y_lows = [lax.all_gather(y_low, "tensor", axis=0)]
    y_recv = hop(y_quad, left)
    half_a = struct((4, 4, 288, 128), BF16)
    g_quad, g_low, keep_a, send_a = call(
        attention_backward,
        "attention_backward",
        [qkv, prob, gcontext, row(ln1_gain), small, small_up, gmid, x, n_one, gw_out, w_full],
        [quad_rows, low_rows, half_a, half_a],
        [extended, extended, narrow, narrow, sum_heads, spread_heads, all_rows, pltpu.VMEM((3, D, D), BF16)]
        + [low_extended, pltpu.VMEM((ROWS, D), F32), rows_low, rows_low, square, weights]
        + [pltpu.VMEM((ROWS, 128), F32), sems((5,))],
        60000000,
        far_ins=(6, 7, 8, 9, 10),
    )
    parts_b = after([both_b[0]] + [to_peer(both_b[k], 2 * k) for k in (1, 2, 3)], keep_a)
    far_a = to_peer(after(send_a, y_recv, *y_lows, *parts_b), 1)
    plane_b = wider([lower([v[s] for v in parts_b]) for s in range(4)])
    mine_b = lax.psum_scatter(jnp.concatenate(plane_b), "tensor", scatter_dimension=0, tiled=True)
    both_a = lower([keep_a, far_a])
    parts_a = lax.all_to_all(both_a, "dp", 0, 0, axis_index_groups=planes, tiled=True)
    g_lows = [hop(after(g_low, both_a), [(w, 3)]) for w in range(3)]
    g_recv = hop(after(g_quad, both_a), left)
    output = call(
        spread_rows, "spread_rows", [after(y_quad, both_a), y_low, y_recv] + y_lows, [struct((SHARD, D), BF16)]
    )[0]
    parts_a = after(parts_a, g_recv, output, *g_lows)
    plane_a = wider([lower([parts_a[i, s] for i in range(4)]) for s in range(4)])
    mine_b = after(mine_b, parts_a)
    flat_b = lax.all_gather(mine_b, "dp", axis=0, axis_index_groups=eights)
    mine_a = lower([plane_a[0]] + [across(plane_a[s], s) for s in (1, 2, 3)])
    grad_tokens = call(
        spread_rows, "spread_rows", [after(g_quad, parts_a), g_low, g_recv] + g_lows, [struct((SHARD, D), F32)]
    )[0]
    mine_a = after(mine_a, output, grad_tokens, mine_b)
    flat_a = lax.all_gather(mine_a, "dp", axis=0, axis_index_groups=eights)
    g_qkv, g_out, g_up, g_down = call(
        unpack_weights,
        "unpack_weights",
        [flat_a, flat_b],
        [struct((3, D, 128), F32), struct((128, D), F32), struct((D, D), F32), struct((D, D), F32)],
        [pltpu.VMEM((3, D, 128), F32), pltpu.VMEM((128, D), F32)] + [pltpu.VMEM((D, D), F32)] * 3 + [sems((4,))],
        far_outs=(0, 1, 2, 3),
    )
    sums = mine_a[256:284].astype(F32).reshape(7, D)
    return (
        output,
        grad_tokens,
        sums[4],
        sums[5],
        g_qkv,
        g_out,
        sums[3],
        sums[1],
        sums[2],
        g_up,
        sums[6],
        g_down,
        sums[0],
    )


def solution(mesh):
    n_dp = mesh.shape["dp"]
    placed = (
        P(("dp", "tensor"), None),
        P(("dp", "tensor"), None),
        P("dp"),
        P("dp", None),
        P(),
        P(),
        P(None, None, "tensor"),
        P("tensor", None),
        P(),
        P(),
        P(),
        P(None, "tensor"),
        P("tensor"),
        P("tensor", None),
        P(),
    )

    def run(*args):
        return shards(*args, n_dp)

    return jax.shard_map(
        run,
        mesh=mesh,
        in_specs=placed,
        out_specs=(
            P(("dp", "tensor"), None),
            P(("dp", "tensor"), None),
            P(),
            P(),
            P(None, None, "tensor"),
            P("tensor", None),
            P(),
            P(),
            P(),
            P(None, "tensor"),
            P("tensor"),
            P("tensor", None),
            P(),
        ),
        check_vma=False,
    )
```
